128 devices in a mesh: item: 8 (over x_lo, z), user: 16 (over x_hi, y, core).
Axes of the slice: x: 4 (x_hi: 2, x_lo: 2; x = x_hi * 2 + x_lo), y: 4, z: 4, core: 2. Of those that a mesh axis runs over, the one named last changes fastest.
Arguments:
- history: bfloat16 [128, 1024, 512], P(('item', 'user')), may hold values from -6 to 6
- hist_len: int32 [128], P(('item', 'user')), may hold values from 256 to 1024, as said below
- cand_ids: int32 [128, 128], P(('item', 'user')), may hold values from 0 to 383, as said below
- cand_lists: int32 [128, 4], P(('item', 'user')), may hold values from 0 to 15, as said below
- item_table: bfloat16 [6144, 512], P('user', 'item'), may hold values from -6 to 6
- w_in: bfloat16 [512, 2048], replicated, may hold values from -0.25 to 0.25
- w_out: bfloat16 [512, 512], replicated, may hold values from -0.25 to 0.25
- grad_cand: bfloat16 [128, 128, 512], P(('item', 'user')), may hold values from -6 to 6
Outputs:
- hist_out: bfloat16 [128, 1024, 512], P(('item', 'user'))
- cand_out: bfloat16 [128, 128, 512], P(('item', 'user'))
- table_grad: float32 [6144, 512], P('user', 'item')
The draws below stay inside these ranges and needn't reach their ends.
Inputs may be any that keep to these rules, and one draw needn't show every extreme that they name: `hist_len`: some user has exactly 1024 events; positions at or past a user's length are padding. `cand_ids`: the 128 ids of one user are different. `cand_lists`: the 4 entries of user g are different and none equals g mod 16.
All inputs are finite; a program needn't handle non-finite values.
Results may differ from the reference program's by a relative error of at most 0.013.
Values may be sent and summed in bfloat16 or wider, within the bound.
A program may use at most 64 MiB of HBM per device.

```python
import jax
import jax.numpy as jnp
from jax import lax

D = 512
H = 8
DH = 64
L = 1024
CAND = 128
NLIST = 4
VB = 384
USERS = 128
VOCAB = 6144
N_USER = 16


def draw_hist_len(key, part):
    key = jax.random.fold_in(key, 11)
    first_key, second_key = jax.random.split(key)
    lengths = jax.random.randint(first_key, (USERS,), L // 4, L + 1)
    longest = jax.random.randint(second_key, (), 0, USERS)
    return jnp.where(jnp.arange(USERS) == longest, L, lengths).astype(jnp.int32)


def draw_cand_ids(key, part):
    key = jax.random.fold_in(key, 23)
    user_keys = jax.random.split(key, USERS)

    def one_row(row_key):
        return jax.random.permutation(row_key, VB)[:CAND]
    return jax.vmap(one_row)(user_keys).astype(jnp.int32)


def draw_cand_lists(key, part):
    key = jax.random.fold_in(key, 37)
    user_keys = jax.random.split(key, USERS)

    def one_row(row_key):
        return jax.random.permutation(row_key, N_USER - 1)[:NLIST] + 1
    offsets = jax.vmap(one_row)(user_keys)
    owners = jnp.arange(USERS) % N_USER
    return ((owners[:, None] + offsets) % N_USER).astype(jnp.int32)


def levels(rng, dims, pieces, low, largest):
    factor_of = 1.0
    for dim, blocks in pieces:
        draws = jax.random.uniform(jax.random.fold_in(jax.random.fold_in(rng, 6), dim), (blocks,), jnp.float32, low / len(pieces), largest / len(pieces))
        factor_of = factor_of * jnp.repeat(jnp.exp(draws), dims[dim] // blocks).reshape((-1,) + (1,) * (len(dims) - 1 - dim))
    return factor_of


def scatter_about(stream_key, shape, spread, limit, cuts=(), held_as=jnp.bfloat16):
    result = spread * jax.random.normal(stream_key, shape, jnp.float32)
    if cuts:
        result = result * levels(stream_key, shape, cuts, -0.22, 0.18)
    return jnp.clip(result, -limit, limit).astype(held_as)


def setup_inputs(seed: int = 0) -> dict:
    seeds = jax.random.split(jax.random.key(seed), 9)
    history = scatter_about(seeds[0], (USERS, L, D), 1.0, 6.0, ((0, 128),))
    hist_len = draw_hist_len(jax.random.fold_in(seeds[8], 71), 0)
    cand_ids = draw_cand_ids(jax.random.fold_in(seeds[8], 71), 0)
    cand_lists = draw_cand_lists(jax.random.fold_in(seeds[8], 71), 0)
    item_table = scatter_about(seeds[4], (VOCAB, D), 1.0, 6.0, ((0, 16), (1, 8)))
    w_in = scatter_about(seeds[5], (D, 4 * D), D ** -0.5, 0.25)
    w_out = scatter_about(seeds[6], (D, D), D ** -0.5, 0.25)
    grad_cand = scatter_about(seeds[7], (USERS, CAND, D), 1.0, 6.0, ((0, 128),))
    return {"history": history, "hist_len": hist_len, "cand_ids": cand_ids, "cand_lists": cand_lists, "item_table": item_table, "w_in": w_in, "w_out": w_out, "grad_cand": grad_cand}


NORM_EPS = 1e-05

def silu_slope(pre_act):
    sigmoid = jax.nn.sigmoid(pre_act)
    return sigmoid * (1.0 + pre_act * (1.0 - sigmoid))

def normalize(rows_in):
    centred = rows_in - lax.optimization_barrier(jnp.mean(rows_in, axis=-1, keepdims=True))
    inv_dev = lax.rsqrt(lax.optimization_barrier(jnp.mean(centred * centred, axis=-1, keepdims=True)) + NORM_EPS)
    return (centred * inv_dev, inv_dev)

def rounded(values):
    return lax.optimization_barrier(values.astype(jnp.bfloat16)).astype(jnp.float32)

def history_user(events, length, w_in, w_out):
    projected = jax.nn.silu(jnp.dot(events, w_in, preferred_element_type=jnp.float32)).astype(jnp.bfloat16)
    u_part = projected[:, :D]
    v_part = projected[:, D:2 * D]
    q_part = projected[:, 2 * D:3 * D]
    k_part = projected[:, 3 * D:]
    heads_q = q_part.astype(jnp.float32).reshape(L, H, DH)
    heads_k = k_part.astype(jnp.float32).reshape(L, H, DH)
    heads_v = v_part.astype(jnp.float32).reshape(L, H, DH)
    scores = jnp.einsum('qhd,khd->hqk', heads_q, heads_k) * DH ** (-0.5)
    positions = jnp.arange(L)
    allowed = (positions[None, :] <= positions[:, None]) & (positions[None, :] < length)
    weights = rounded(jnp.where(allowed[None], jax.nn.silu(scores), 0.0))
    attended = jnp.einsum('hqk,khd->qhd', weights, heads_v).reshape(L, D)
    normed = normalize(attended)[0]
    mixed_rows = (normed * u_part.astype(jnp.float32)).astype(jnp.bfloat16)
    layer_out = jnp.dot(mixed_rows, w_out, preferred_element_type=jnp.float32) + events.astype(jnp.float32)
    layer_out = jnp.where((positions < length)[:, None], layer_out, 0.0).astype(jnp.bfloat16)
    return (layer_out, k_part, v_part)

def candidate_pass(cand_q, cand_u, cand_emb, keys_k, keys_v, valid_keys, w_out, grad_rows):
    att_scale = DH ** (-0.5)
    heads_q = cand_q.astype(jnp.float32).reshape(CAND, H, DH)
    heads_k = keys_k.astype(jnp.float32).reshape(-1, H, DH)
    heads_v = keys_v.astype(jnp.float32).reshape(-1, H, DH)
    scores = jnp.einsum('qhd,khd->hqk', heads_q, heads_k) * att_scale
    weights = rounded(jnp.where(valid_keys[None, None, :], jax.nn.silu(scores), 0.0))
    attended = jnp.einsum('hqk,khd->qhd', weights, heads_v).reshape(CAND, D)
    normed, inv_dev = normalize(attended)
    u_rows = cand_u.astype(jnp.float32)
    mixed_rows = (normed * u_rows).astype(jnp.bfloat16)
    layer_out = (jnp.dot(mixed_rows, w_out, preferred_element_type=jnp.float32) + cand_emb.astype(jnp.float32)).astype(jnp.bfloat16)
    grad_mixed = jnp.dot(grad_rows, w_out.T, preferred_element_type=jnp.float32)
    grad_u = grad_mixed * normed
    grad_normed = grad_mixed * u_rows
    grad_att = inv_dev * (grad_normed - lax.optimization_barrier(jnp.mean(grad_normed, axis=-1, keepdims=True)) - normed * lax.optimization_barrier(jnp.mean(grad_normed * normed, axis=-1, keepdims=True)))
    grad_att = rounded(grad_att).reshape(CAND, H, DH)
    grad_weights = jnp.einsum('qhd,khd->hqk', grad_att, heads_v)
    grad_scores = rounded(jnp.where(valid_keys[None, None, :], grad_weights * silu_slope(scores), 0.0) * att_scale)
    grad_q = jnp.einsum('hqk,khd->qhd', grad_scores, heads_k).reshape(CAND, D)
    grad_k = jnp.einsum('hqk,qhd->khd', grad_scores[:, :, L:], heads_q).reshape(-1, D)
    grad_v = jnp.einsum('hqk,qhd->khd', weights[:, :, L:], grad_att).reshape(-1, D)
    return (layer_out, grad_u, grad_q, grad_k, grad_v)

def reference(history, hist_len, cand_ids, cand_lists, item_table, w_in, w_out, grad_cand):

    def one_user(packed):
        return history_user(packed[0], packed[1], w_in, w_out)
    hist_out, hist_keys, hist_vals = lax.map(one_user, (history, hist_len))
    user_no = jnp.arange(USERS, dtype=jnp.int32)
    table_rows = (user_no % N_USER * VB)[:, None] + cand_ids
    cand_emb = item_table[table_rows]
    cand_pre = jnp.dot(cand_emb.reshape(USERS * CAND, D), w_in, preferred_element_type=jnp.float32).reshape(USERS, CAND, 4 * D)
    cand_proj = jax.nn.silu(cand_pre).astype(jnp.bfloat16)
    cand_u = cand_proj[:, :, :D]
    cand_v = cand_proj[:, :, D:2 * D]
    cand_q = cand_proj[:, :, 2 * D:3 * D]
    cand_k = cand_proj[:, :, 3 * D:]
    listed = (user_no // N_USER * N_USER)[:, None] + cand_lists
    key_valid = jnp.ones(((1 + NLIST) * CAND,), dtype=bool)
    positions = jnp.arange(L)

    def one_cand(packed):
        owner_no, keys_hist, vals_hist, length = packed
        picked = listed[owner_no]
        keys_k = jnp.concatenate([keys_hist, cand_k[owner_no], cand_k[picked].reshape(NLIST * CAND, D)], 0)
        keys_v = jnp.concatenate([vals_hist, cand_v[owner_no], cand_v[picked].reshape(NLIST * CAND, D)], 0)
        valid_keys = jnp.concatenate([positions < length, key_valid], 0)
        return candidate_pass(cand_q[owner_no], cand_u[owner_no], cand_emb[owner_no], keys_k, keys_v, valid_keys, w_out, grad_cand[owner_no])
    cand_out, grad_u, grad_q, grad_k, grad_v = lax.map(one_cand, (user_no, hist_keys, hist_vals, hist_len))
    total_k = grad_k[:, :CAND].at[listed].add(grad_k[:, CAND:].reshape(USERS, NLIST, CAND, D))
    total_v = grad_v[:, :CAND].at[listed].add(grad_v[:, CAND:].reshape(USERS, NLIST, CAND, D))
    grad_proj = jnp.concatenate([grad_u, total_v, grad_q, total_k], -1)
    grad_pre = (grad_proj * silu_slope(cand_pre)).astype(jnp.bfloat16)
    grad_emb = jnp.dot(grad_pre.reshape(USERS * CAND, 4 * D), w_in.T, preferred_element_type=jnp.float32)
    grad_emb = grad_emb + grad_cand.reshape(USERS * CAND, D).astype(jnp.float32)
    table_grad = jnp.zeros((VOCAB, D), jnp.float32).at[table_rows.reshape(-1)].add(grad_emb)
    return (hist_out, cand_out, table_grad)
```

```python
import functools

import jax
import jax.numpy as jnp
from jax import lax
from jax.experimental import pallas as pl
from jax.experimental.pallas import tpu as pltpu
from jax.sharding import PartitionSpec as P

H = 8
GROUP = 4
NORM_EPS = 1e-05
QB = 256
MESH = pl.DeviceIdType.MESH

F32 = jnp.float32
BF16 = jnp.bfloat16


def nn(a, b):
    return lax.dot_general(a, b, (((1,), (0,)), ((), ())), preferred_element_type=F32)


def nt(a, b):
    return lax.dot_general(a, b, (((1,), (1,)), ((), ())), preferred_element_type=F32)


def tn(a, b):
    return lax.dot_general(a, b, (((0,), (0,)), ((), ())), preferred_element_type=F32)


def silu(v):
    half = 0.5 * v
    return half + half * jnp.tanh(half)


def silu_slope(v):
    half = 0.5 * v
    sig = 0.5 + 0.5 * jnp.tanh(half)
    return sig + (v * sig) * (1.0 - sig)


def head_lane(shape, h):
    lane = lax.broadcasted_iota(jnp.int32, shape, len(shape) - 1)
    width = shape[-1] // GROUP
    return (lane >= h * width) & (lane < (h + 1) * width)


def only_head(x, h):
    return jnp.where(head_lane(x.shape, h), x, jnp.zeros_like(x))


def stacked_heads(x):
    return jnp.concatenate([only_head(x, h) for h in range(GROUP)], 0)


def unstacked_heads(x):
    rows = x.shape[0] // GROUP
    total = only_head(x[:rows], 0)
    for h in range(1, GROUP):
        total = total + only_head(x[h * rows : (h + 1) * rows], h)
    return total


def kernel(
    len_ref, lists_ref, ids_ref, table_ref, hist_hbm, win_hbm, wout_hbm, gcand_hbm,
    hist_out, cand_out, tgrad_out,
    hist, win, wout, gcand,
    tab, ids, table, u2, q2, k2, v2, att, outv,
    emb, pre_own, pre_slot, uc, qc, gmix, gatt, wts, slope, gq, gkv, gown,
    contrib, send_back, recv_back, gsend, grecv, coutv, tgv,
    local_sem, out_sem, tab_send, tab_recv, ids_send, ids_recv,
    emb_send, emb_recv, back_send, back_recv, fin_send, fin_recv,
):
    n_item = lax.axis_size("item")
    n_user = lax.axis_size("user")
    me_i = lax.axis_index("item")
    me_u = lax.axis_index("user")
    rows, d = hist.shape
    cand = gcand.shape[0]
    vb, piece = table_ref.shape
    half_vb = vb // 2
    half_cand = cand // 2
    gw = d // 2
    n_slot = contrib.shape[0] - 1
    n_key = k2.shape[1]
    scale = (d // H) ** (-0.5)
    barrier = pltpu.get_barrier_semaphore()

    copies = [
        pltpu.make_async_copy(hist_hbm, hist, local_sem.at[0]),
        pltpu.make_async_copy(win_hbm, win, local_sem.at[1]),
        pltpu.make_async_copy(gcand_hbm, gcand, local_sem.at[2]),
        pltpu.make_async_copy(wout_hbm, wout, local_sem.at[3]),
    ]
    for c in copies:
        c.start()

    def peer_i(k):
        return {"item": lax.rem(me_i + k, n_item)}

    def peer_u(k):
        return {"user": lax.rem(me_u + k, n_user)}

    @pl.loop(1, n_item)
    def _(k):
        pl.semaphore_signal(barrier, inc=1, device_id=peer_i(k), device_id_type=MESH)

    @pl.loop(1, n_user)
    def _(k):
        pl.semaphore_signal(barrier, inc=1, device_id=peer_u(k), device_id_type=MESH)

    tab[me_i] = jnp.concatenate([table_ref[:half_vb], table_ref[half_vb:]], 1)
    ids[me_i] = jnp.broadcast_to(ids_ref[...], ids.shape[1:])
    pl.semaphore_wait(barrier, n_item + n_user - 2)

    def tab_copy(k):
        return pltpu.make_async_remote_copy(
            src_ref=tab.at[me_i], dst_ref=tab.at[me_i], send_sem=tab_send.at[k],
            recv_sem=tab_recv.at[k], device_id=peer_i(k), device_id_type=MESH)

    def ids_copy(k):
        return pltpu.make_async_remote_copy(
            src_ref=ids.at[me_i], dst_ref=ids.at[me_i], send_sem=ids_send.at[k],
            recv_sem=ids_recv.at[k], device_id=peer_i(k), device_id_type=MESH)

    def emb_copy(k):
        return pltpu.make_async_remote_copy(
            src_ref=emb.at[me_u], dst_ref=emb.at[me_u], send_sem=emb_send.at[k],
            recv_sem=emb_recv.at[k], device_id=peer_u(k), device_id_type=MESH)

    def back_copy(k):
        return pltpu.make_async_remote_copy(
            src_ref=send_back.at[k], dst_ref=recv_back.at[k], send_sem=back_send.at[k],
            recv_sem=back_recv.at[k], device_id=peer_u(k), device_id_type=MESH)

    def fin_copy(k):
        return pltpu.make_async_remote_copy(
            src_ref=gsend.at[lax.rem(me_i + k, n_item)], dst_ref=grecv.at[me_i],
            send_sem=fin_send.at[k], recv_sem=fin_recv.at[k],
            device_id=peer_i(k), device_id_type=MESH)

    @pl.loop(1, n_item)
    def _(k):
        tab_copy(k).start()
        ids_copy(k).start()

    length = len_ref[0]
    copies[0].wait()
    copies[1].wait()

    @pl.loop(0, rows // QB)
    def _(b):
        at = pl.ds(pl.multiple_of(b * QB, QB), QB)
        x = hist[at]
        keep = (b * QB + lax.broadcasted_iota(jnp.int32, (QB, 1), 0)) < length
        for g in range(2):
            c = g * gw
            u2[g, at] = silu(nn(x, win[:, c : c + gw])).astype(BF16)
            val = silu(nn(x, win[:, d + c : d + c + gw]))
            v2[g, at] = jnp.where(keep, val, 0.0).astype(BF16)
            q2[g, at] = silu(nn(x, win[:, 2 * d + c : 2 * d + c + gw])).astype(BF16) * (scale / 2)
            k2[g, at] = silu(nn(x, win[:, 3 * d + c : 3 * d + c + gw])).astype(BF16)

    @pl.loop(1, n_item)
    def _(k):
        tab_copy(k).wait_recv()
        ids_copy(k).wait_recv()

    for j in range(tab.shape[0]):
        t = tab[j]
        table[:half_vb, j * piece : (j + 1) * piece] = t[:, :piece]
        table[half_vb:, j * piece : (j + 1) * piece] = t[:, piece:]

    def hot(ids_row):
        row = lax.broadcasted_iota(jnp.int32, (vb, cand), 0)
        return jnp.where(row == ids_row, 1.0, 0.0).astype(BF16)

    own = tn(hot(ids_ref[...]), table[...]).astype(BF16)
    emb[me_u] = own

    @pl.loop(1, n_user)
    def _(k):
        emb_copy(k).start()

    copies[2].wait()
    copies[3].wait()

    pre_own[...] = nn(own, win[...])
    for g in range(2):
        c = g * gw
        uc[g] = silu(pre_own[:, c : c + gw]).astype(BF16)
        v2[g, rows : rows + cand] = silu(pre_own[:, d + c : d + c + gw]).astype(BF16)
        qc[g] = silu(pre_own[:, 2 * d + c : 2 * d + c + gw]).astype(BF16) * (scale / 2)
        k2[g, rows : rows + cand] = silu(pre_own[:, 3 * d + c : 3 * d + c + gw]).astype(BF16)
    gmix[...] = nt(gcand[...], wout[...])

    def normalize(a0, a1):
        mean = (jnp.sum(a0, 1, keepdims=True) + jnp.sum(a1, 1, keepdims=True)) / d
        a0 = a0 - mean
        a1 = a1 - mean
        var = (jnp.sum(a0 * a0, 1, keepdims=True) + jnp.sum(a1 * a1, 1, keepdims=True)) / d
        inv = lax.rsqrt(var + NORM_EPS)
        return a0 * inv, a1 * inv, inv

    def history_block(b):
        lo = b * QB
        n = lo + QB

        @pl.loop(0, 2)
        def _(g):
            q = q2[g, lo:n]
            key = k2[g, :n]
            val = v2[g, :n]
            total = jnp.zeros((QB, gw), F32)
            for h in range(GROUP):
                y = nt(only_head(q, h), key)
                w = y + y * jnp.tanh(y)
                last = w[:, lo:]
                r = lax.broadcasted_iota(jnp.int32, (QB, QB), 0)
                c = lax.broadcasted_iota(jnp.int32, (QB, QB), 1)
                last = jnp.where(c <= r, last, 0.0).astype(BF16)
                if b:
                    w = jnp.concatenate([w[:, :lo].astype(BF16), last], 1)
                else:
                    w = last
                total = total + only_head(nn(w, val), h)
            att[g] = total

        n0, n1, _ = normalize(att[0], att[1])
        m0 = (n0 * u2[0, lo:n].astype(F32)).astype(BF16)
        m1 = (n1 * u2[1, lo:n].astype(F32)).astype(BF16)
        out = nn(m0, wout[:gw]) + nn(m1, wout[gw:]) + hist[lo:n].astype(F32)
        keep = (lo + lax.broadcasted_iota(jnp.int32, (QB, 1), 0)) < length
        outv[lo:n] = jnp.where(keep, out, 0.0).astype(BF16)
        copy = pltpu.make_async_copy(
            outv.at[pl.ds(lo, QB)], hist_out.at[pl.ds(lo, QB)], out_sem.at[b])
        copy.start()
        return copy

    outs = [history_block(3), history_block(0)]

    @pl.loop(1, n_user)
    def _(k):
        emb_copy(k).wait_recv()

    @pl.loop(0, n_slot)
    def _(t):
        e = emb[lists_ref[t]]
        at = pl.ds(pl.multiple_of(rows + cand + t * cand, cand), cand)
        for g in range(2):
            c = g * gw
            pv = nn(e, win[:, d + c : d + c + gw])
            pk = nn(e, win[:, 3 * d + c : 3 * d + c + gw])
            pre_slot[t, :, c : c + gw] = pv
            pre_slot[t, :, d + c : d + c + gw] = pk
            v2[g, at] = silu(pv).astype(BF16)
            k2[g, at] = silu(pk).astype(BF16)

    @pl.loop(0, 2)
    def _(g):
        y = nt(stacked_heads(qc[g]), k2[g])
        t = jnp.tanh(y)
        w = y + y * t
        p = 0.5 + 0.5 * t
        slope[g] = p + w * (1.0 - p)
        wb = w.astype(BF16)
        wts[g] = wb
        att[g, :cand] = unstacked_heads(nn(wb, v2[g]))

    n0, n1, inv = normalize(att[0, :cand], att[1, :cand])
    uc0 = uc[0].astype(F32)
    uc1 = uc[1].astype(F32)
    m0 = (n0 * uc0).astype(BF16)
    m1 = (n1 * uc1).astype(BF16)
    coutv[...] = (nn(m0, wout[:gw]) + nn(m1, wout[gw:]) + own.astype(F32)).astype(BF16)
    cout_copy = pltpu.make_async_copy(coutv, cand_out, out_sem.at[4])
    cout_copy.start()
    gm0 = gmix[:, :gw]
    gm1 = gmix[:, gw:]
    gn0 = gm0 * uc0
    gn1 = gm1 * uc1
    mean_g = (jnp.sum(gn0, 1, keepdims=True) + jnp.sum(gn1, 1, keepdims=True)) / d
    mean_gn = (jnp.sum(gn0 * n0, 1, keepdims=True) + jnp.sum(gn1 * n1, 1, keepdims=True)) / d
    gatt[0] = (inv * (gn0 - mean_g - n0 * mean_gn)).astype(BF16)
    gatt[1] = (inv * (gn1 - mean_g - n1 * mean_gn)).astype(BF16)
    gmix[:, :gw] = gm0 * n0
    gmix[:, gw:] = gm1 * n1

    @pl.loop(0, 2)
    def _(g):
        ga = stacked_heads(gatt[g])
        gwt = nt(ga, v2[g])
        gs = (gwt * slope[g] * scale).astype(BF16)
        gq[g] = unstacked_heads(nn(gs, k2[g]))
        gkv[0, g] = tn(gs[:, rows:], stacked_heads(qc[g])) * (2.0 / scale)
        gkv[1, g] = tn(wts[g, :, rows:], ga)

    @pl.loop(0, n_slot)
    def _(t):
        at = pl.ds(pl.multiple_of(cand + t * cand, cand), cand)
        total = jnp.zeros((cand, d), F32)
        for g in range(2):
            c = g * gw
            dk = (gkv[0, g, at] * silu_slope(pre_slot[t, :, d + c : d + c + gw])).astype(BF16)
            dv = (gkv[1, g, at] * silu_slope(pre_slot[t, :, c : c + gw])).astype(BF16)
            total = total + nt(dv, win[:, d + c : d + c + gw])
            total = total + nt(dk, win[:, 3 * d + c : 3 * d + c + gw])
        contrib[t] = total.astype(BF16)

    contrib[n_slot] = jnp.zeros((cand, d), BF16)

    @pl.loop(1, n_user)
    def _(k):
        owner = lax.rem(me_u + k, n_user)
        slot = n_slot
        for t in range(n_slot):
            slot = jnp.where(lists_ref[t] == owner, t, slot)
        send_back[k] = contrib[slot]
        back_copy(k).start()

    total = gcand[...].astype(F32)
    for g in range(2):
        c = g * gw
        for part, grad in (
            (0, gmix[:, c : c + gw]),
            (1, gkv[1, g, :cand]),
            (2, gq[g]),
            (3, gkv[0, g, :cand]),
        ):
            col = part * d + c
            dp = (grad * silu_slope(pre_own[:, col : col + gw])).astype(BF16)
            total = total + nt(dp, win[:, col : col + gw])
    gown[...] = total

    outs += [history_block(2), history_block(1)]

    @pl.loop(1, n_user)
    def _(k):
        back_copy(k).wait_recv()
        gown[...] += recv_back[k].astype(F32)

    g_all = gown[...].astype(BF16)
    for j in range(tab.shape[0]):
        x = g_all[:, j * piece : (j + 1) * piece]
        gsend[j] = jnp.concatenate([x[:half_cand], x[half_cand:]], 1)
    grecv[me_i] = gsend[me_i]

    @pl.loop(1, n_item)
    def _(k):
        fin_copy(k).start()

    @pl.loop(1, n_item)
    def _(k):
        fin_copy(k).wait_recv()

    tg = jnp.zeros((vb, piece), F32)
    for j in range(tab.shape[0]):
        x = grecv[j]
        x = jnp.concatenate([x[:, :piece], x[:, piece:]], 0)
        tg = tg + nn(hot(ids[j, :1]), x)
    tgv[...] = tg
    tg_copy = pltpu.make_async_copy(tgv, tgrad_out, out_sem.at[5])
    tg_copy.start()

    @pl.loop(1, n_item)
    def _(k):
        tab_copy(k).wait_send()
        ids_copy(k).wait_send()
        fin_copy(k).wait_send()

    @pl.loop(1, n_user)
    def _(k):
        emb_copy(k).wait_send()
        back_copy(k).wait_send()

    for c in outs:
        c.wait()
    cout_copy.wait()
    tg_copy.wait()


def local(history, hist_len, cand_ids, cand_lists, item_table, w_in, w_out, grad_cand):
    rows, d = history.shape[1:]
    cand = cand_ids.shape[1]
    n_slot = cand_lists.shape[1]
    vb, piece = item_table.shape
    n_item = lax.axis_size("item")
    n_user = lax.axis_size("user")
    gw = d // 2
    n_key = rows + (1 + n_slot) * cand
    vmem = pl.BlockSpec(memory_space=pltpu.VMEM)
    smem = pl.BlockSpec(memory_space=pltpu.SMEM)
    hbm = pl.BlockSpec(memory_space=pl.ANY)
    V = pltpu.VMEM
    dma = pltpu.SemaphoreType.DMA
    hist_out, cand_out, tgrad = pl.pallas_call(
        kernel,
        out_shape=(
            jax.ShapeDtypeStruct((rows, d), BF16),
            jax.ShapeDtypeStruct((cand, d), BF16),
            jax.ShapeDtypeStruct((vb, piece), F32),
        ),
        in_specs=[smem, smem, vmem, vmem, hbm, hbm, hbm, hbm],
        out_specs=(hbm, hbm, hbm),
        scratch_shapes=[
            V((rows, d), BF16), V((d, 4 * d), BF16), V((d, d), BF16), V((cand, d), BF16),
            V((n_item, vb // 2, 2 * piece), BF16), V((n_item, 8, cand), jnp.int32),
            V((vb, d), BF16),
            V((2, rows, gw), BF16), V((2, rows, gw), BF16),
            V((2, n_key, gw), BF16), V((2, n_key, gw), BF16),
            V((2, QB, gw), F32), V((rows, d), BF16),
            V((n_user, cand, d), BF16), V((cand, 4 * d), F32), V((n_slot, cand, 2 * d), F32),
            V((2, cand, gw), BF16), V((2, cand, gw), BF16), V((cand, d), F32),
            V((2, cand, gw), BF16),
            V((2, GROUP * cand, n_key), BF16), V((2, GROUP * cand, n_key), F32),
            V((2, cand, gw), F32), V((2, 2, (1 + n_slot) * cand, gw), F32), V((cand, d), F32),
            V((n_slot + 1, cand, d), BF16), V((n_user, cand, d), BF16),
            V((n_user, cand, d), BF16),
            V((n_item, cand // 2, 2 * piece), BF16), V((n_item, cand // 2, 2 * piece), BF16),
            V((cand, d), BF16), V((vb, piece), F32),
            dma((4,)), dma((6,)),
            dma((n_item,)), dma((n_item,)), dma((n_item,)), dma((n_item,)),
            dma((n_user,)), dma((n_user,)), dma((n_user,)), dma((n_user,)),
            dma((n_item,)), dma((n_item,)),
        ],
        compiler_params=pltpu.CompilerParams(
            collective_id=0, has_side_effects=True, vmem_limit_bytes=56 * 1024 * 1024),
    )(
        hist_len, cand_lists[0], cand_ids, item_table, history[0], w_in, w_out, grad_cand[0],
    )
    return hist_out[None], cand_out[None], tgrad


def solution(mesh):
    in_specs = (
        P(("item", "user"), None, None),
        P(("item", "user")),
        P(("item", "user"), None),
        P(("item", "user"), None),
        P("user", "item"),
        P(),
        P(),
        P(("item", "user"), None, None),
    )
    out_specs = (
        P(("item", "user"), None, None),
        P(("item", "user"), None, None),
        P("user", "item"),
    )
    return jax.shard_map(local, mesh=mesh, in_specs=in_specs, out_specs=out_specs, check_vma=False)
```

```python
import functools

import jax
import jax.numpy as jnp
from jax import lax
from jax.experimental import pallas as pl
from jax.experimental.pallas import tpu as pltpu
from jax.sharding import PartitionSpec as P

H = 8
GROUP = 4
NORM_EPS = 1e-05
QB = 256
MESH = pl.DeviceIdType.MESH

F32 = jnp.float32
BF16 = jnp.bfloat16


def nn(a, b):
    return lax.dot_general(a, b, (((1,), (0,)), ((), ())), preferred_element_type=F32)


def nt(a, b):
    return lax.dot_general(a, b, (((1,), (1,)), ((), ())), preferred_element_type=F32)


def tn(a, b):
    return lax.dot_general(a, b, (((0,), (0,)), ((), ())), preferred_element_type=F32)


def silu(v):
    half = 0.5 * v
    return half + half * jnp.tanh(half)


def silu_slope(v):
    half = 0.5 * v
    sig = 0.5 + 0.5 * jnp.tanh(half)
    return sig + (v * sig) * (1.0 - sig)


def head_lane(shape, h):
    lane = lax.broadcasted_iota(jnp.int32, shape, len(shape) - 1)
    width = shape[-1] // GROUP
    return (lane >= h * width) & (lane < (h + 1) * width)


def only_head(x, h):
    return jnp.where(head_lane(x.shape, h), x, jnp.zeros_like(x))


def stacked_heads(x):
    return jnp.concatenate([only_head(x, h) for h in range(GROUP)], 0)


def unstacked_heads(x):
    rows = x.shape[0] // GROUP
    total = only_head(x[:rows], 0)
    for h in range(1, GROUP):
        total = total + only_head(x[h * rows : (h + 1) * rows], h)
    return total


def kernel(
    len_ref, lists_ref, ids_ref, table_hbm, hist_hbm, win_hbm, wout_hbm, gcand_hbm,
    hist_out, cand_out, tgrad_out, *,
    hist, win, wout, gcand, tabc, tags, tags_i, pick, back, hotc, e_all, disp, eown, eslot,
    u2, q2, k2, v2, att, catt, outv, pre_own, pre_slot, uc, qc, gmix, gatt, wts, slope, gq, gkv,
    dsend, drecv, share, share_in, csum, fin, coutv, tgv,
    local_sem, out_sem, s_tab, r_tab, s_tag, r_tag, s_tagi, r_tagi, s_own, r_own, s_slot, r_slot,
    s_back, r_back, s_share, r_share, s_fin, r_fin,
):
    n_item = lax.axis_size("item")
    n_user = lax.axis_size("user")
    me_i = lax.axis_index("item")
    me_u = lax.axis_index("user")
    rows, d = hist.shape
    cand = gcand.shape[0]
    chunk, vb = tabc.shape[1:]
    piece = table_hbm.shape[0]
    per = piece // chunk
    gw = d // 2
    n_slot = eslot.shape[1] // chunk
    own_end = rows + cand
    scale = (d // H) ** (-0.5)
    barrier = pltpu.get_barrier_semaphore()
    holder = me_u // per
    at_home = holder == me_i

    copies = [
        pltpu.make_async_copy(hist_hbm, hist, local_sem.at[0]),
        pltpu.make_async_copy(win_hbm, win, local_sem.at[1]),
        pltpu.make_async_copy(gcand_hbm, gcand, local_sem.at[2]),
        pltpu.make_async_copy(wout_hbm, wout, local_sem.at[3]),
    ]

    def peer_i(k):
        return {"item": lax.rem(me_i + k, n_item)}

    def peer_u(k):
        return {"user": lax.rem(me_u + k, n_user)}

    def worker(n):
        return (lax.rem(me_i + n // per, n_item), me_i * per + lax.rem(n, per))

    def not_me(place):
        return jnp.logical_or(place[0] != me_i, place[1] != me_u)

    def signal(place):
        pl.semaphore_signal(barrier, inc=1, device_id=place, device_id_type=MESH)

    @pl.loop(1, n_item)
    def _(k):
        signal(peer_i(k))

    @pl.loop(1, n_user)
    def _(k):
        signal(peer_u(k))

    @pl.loop(0, n_user)
    def _(n):
        @pl.when(not_me(worker(n)))
        def _():
            signal(worker(n))

        @pl.when(not_me((holder, n)))
        def _():
            signal((holder, n))

    for c in copies:
        c.start()

    lane = lax.broadcasted_iota(jnp.int32, (1, cand), 1)
    key_row = jnp.zeros((1, cand), jnp.int32)
    for t in range(n_slot):
        key_row = jnp.where(lane // chunk == t, lists_ref[t] * chunk + lane - t * chunk, key_row)
    tag = jnp.concatenate([ids_ref[...], key_row, jnp.zeros((6, cand), jnp.int32)], 0)
    tags[me_u] = tag
    tags_i[me_i] = tag

    def remote(src, dst, send, recv, place):
        return pltpu.make_async_remote_copy(
            src_ref=src, dst_ref=dst, send_sem=send, recv_sem=recv, device_id=place,
            device_id_type=MESH)

    def tag_copy(k):
        return remote(tags.at[me_u], tags.at[me_u], s_tag.at[k], r_tag.at[k], peer_u(k))

    def tagi_copy(k):
        return remote(tags_i.at[me_i], tags_i.at[me_i], s_tagi.at[k], r_tagi.at[k], peer_i(k))

    def tab_copy(n):
        at = pl.ds(pl.multiple_of(lax.rem(n, per) * chunk, chunk), chunk)
        return remote(table_hbm.at[at], tabc.at[me_u], s_tab.at[n], r_tab.at[me_u], worker(n))

    def tab_arrival(u):
        return remote(tabc.at[u], tabc.at[u], s_tab.at[u], r_tab.at[u], (holder, u))

    def own_copy(k):
        to = lax.rem(me_u + k, n_user)
        return remote(e_all.at[to], eown.at[me_u], s_own.at[k], r_own.at[k], peer_u(k))

    def slot_copy(k):
        to = lax.rem(me_u + k, n_user)
        return remote(disp.at[to], eslot.at[me_u], s_slot.at[k], r_slot.at[k], peer_u(k))

    def back_copy(k):
        to = lax.rem(me_u + k, n_user)
        return remote(dsend.at[to], drecv.at[me_u], s_back.at[k], r_back.at[k], peer_u(k))

    def share_copy(k):
        to = lax.rem(me_i + k, n_item)
        return remote(share.at[to], share_in.at[me_i], s_share.at[k], r_share.at[k], peer_i(k))

    def fin_copy(r):
        n = me_i * per + lax.rem(me_u, per)
        return remote(csum.at[r], fin.at[n], s_fin.at[r], r_fin.at[n], (holder, r))

    def fin_arrival(n):
        return remote(fin.at[n], fin.at[n], s_fin.at[n], r_fin.at[n], (n // per, me_i * per + n % per))

    home_at = pl.ds(pl.multiple_of(lax.rem(me_u, per) * chunk, chunk), chunk)
    home_copy = pltpu.make_async_copy(table_hbm.at[home_at], tabc.at[me_u], local_sem.at[4])

    pl.semaphore_wait(
        barrier, n_item + 3 * n_user - 2 - 2 * at_home.astype(jnp.int32))

    @pl.loop(0, n_user)
    def _(n):
        @pl.when(not_me(worker(n)))
        def _():
            tab_copy(n).start()

    @pl.when(at_home)
    def _():
        home_copy.start()

    @pl.loop(1, n_user)
    def _(k):
        tag_copy(k).start()

    @pl.loop(1, n_item)
    def _(k):
        tagi_copy(k).start()

    length = len_ref[0]
    for c in copies:
        c.wait()

    @pl.loop(0, rows // QB)
    def _(b):
        at = pl.ds(pl.multiple_of(b * QB, QB), QB)
        x = hist[at]
        keep = (b * QB + lax.broadcasted_iota(jnp.int32, (QB, 1), 0)) < length
        for g in range(2):
            c = g * gw
            u2[g, at] = silu(nn(x, win[:, c : c + gw])).astype(BF16)
            val = silu(nn(x, win[:, d + c : d + c + gw]))
            v2[g, at] = jnp.where(keep, val, 0.0).astype(BF16)
            q2[g, at] = silu(nn(x, win[:, 2 * d + c : 2 * d + c + gw])).astype(BF16) * (scale / 2)
            k2[g, at] = silu(nn(x, win[:, 3 * d + c : 3 * d + c + gw])).astype(BF16)

    gmix[...] = nt(gcand[...], wout[...])

    @pl.loop(1, n_user)
    def _(k):
        tag_copy(k).wait_recv()

    keys = jnp.concatenate([tags[u, 1:2] for u in range(n_user)], 0)
    keys_t = jnp.transpose(keys.astype(F32)).astype(jnp.int32)
    line = n_slot * chunk
    col = lax.broadcasted_iota(jnp.int32, (line, n_user * chunk), 1)
    row = lax.broadcasted_iota(jnp.int32, (n_user * chunk, line), 0)
    for u in range(n_user):
        pick[u * line : (u + 1) * line] = jnp.where(
            col == keys_t[:, u : u + 1], 1.0, 0.0).astype(BF16)
        back[:, u * line : (u + 1) * line] = jnp.where(
            row == keys[u : u + 1], 1.0, 0.0).astype(BF16)

    @pl.loop(0, n_user)
    def _(u):
        @pl.when(not_me((holder, u)))
        def _():
            tab_arrival(u).wait_recv()

    @pl.when(at_home)
    def _():
        home_copy.wait()

    @pl.loop(0, n_user)
    def _(u):
        at = lax.broadcasted_iota(jnp.int32, (vb, cand), 0)
        hot = jnp.where(at == tags[u, 0:1], 1.0, 0.0).astype(BF16)
        e_all[u] = nn(tabc[u], hot).astype(BF16)

    eown[me_u] = e_all[me_u]

    @pl.loop(1, n_user)
    def _(k):
        own_copy(k).start()

    picked = nn(pick[...], e_all[...].reshape(n_user * chunk, cand)).astype(BF16)
    disp[...] = picked.reshape(disp.shape)
    eslot[me_u] = disp[me_u]

    @pl.loop(1, n_user)
    def _(k):
        slot_copy(k).start()

    def normalize(a0, a1):
        mean = (jnp.sum(a0, 1, keepdims=True) + jnp.sum(a1, 1, keepdims=True)) / d
        a0 = a0 - mean
        a1 = a1 - mean
        var = (jnp.sum(a0 * a0, 1, keepdims=True) + jnp.sum(a1 * a1, 1, keepdims=True)) / d
        inv = lax.rsqrt(var + NORM_EPS)
        return a0 * inv, a1 * inv, inv

    def history_block(b):
        lo = b * QB
        n = lo + QB

        @pl.loop(0, 2)
        def _(g):
            q = q2[g, lo:n]
            key = k2[g, :n]
            val = v2[g, :n]
            total = jnp.zeros((QB, gw), F32)
            for h in range(GROUP):
                y = nt(only_head(q, h), key)
                w = y + y * jnp.tanh(y)
                last = w[:, lo:]
                r = lax.broadcasted_iota(jnp.int32, (QB, QB), 0)
                c = lax.broadcasted_iota(jnp.int32, (QB, QB), 1)
                last = jnp.where(c <= r, last, 0.0).astype(BF16)
                if b:
                    w = jnp.concatenate([w[:, :lo].astype(BF16), last], 1)
                else:
                    w = last
                total = total + only_head(nn(w, val), h)
            att[g] = total

        n0, n1, _ = normalize(att[0], att[1])
        m0 = (n0 * u2[0, lo:n].astype(F32)).astype(BF16)
        m1 = (n1 * u2[1, lo:n].astype(F32)).astype(BF16)
        out = nn(m0, wout[:gw]) + nn(m1, wout[gw:]) + hist[lo:n].astype(F32)
        keep = (lo + lax.broadcasted_iota(jnp.int32, (QB, 1), 0)) < length
        outv[lo:n] = jnp.where(keep, out, 0.0).astype(BF16)
        copy = pltpu.make_async_copy(
            outv.at[pl.ds(lo, QB)], hist_out.at[pl.ds(lo, QB)], out_sem.at[b])
        copy.start()
        return copy

    outs = [history_block(1)]

    @pl.loop(1, n_user)
    def _(k):
        own_copy(k).wait_recv()

    own = jnp.transpose(eown[...].reshape(d, cand).astype(F32)).astype(BF16)
    pre_own[...] = nn(own, win[...])
    for g in range(2):
        c = g * gw
        uc[g] = silu(pre_own[:, c : c + gw]).astype(BF16)
        v2[g, rows:own_end] = silu(pre_own[:, d + c : d + c + gw]).astype(BF16)
        qc[g] = silu(pre_own[:, 2 * d + c : 2 * d + c + gw]).astype(BF16) * (scale / 2)
        k2[g, rows:own_end] = silu(pre_own[:, 3 * d + c : 3 * d + c + gw]).astype(BF16)

    def scores(g, lo, hi):
        y = nt(stacked_heads(qc[g]), k2[g, lo:hi])
        t = jnp.tanh(y)
        w = y + y * t
        p = 0.5 + 0.5 * t
        slope[g, :, lo:hi] = p + w * (1.0 - p)
        wb = w.astype(BF16)
        late = max(lo, rows)
        wts[g, :, late - rows : hi - rows] = wb[:, late - lo :]
        return unstacked_heads(nn(wb, v2[g, lo:hi]))

    @pl.loop(0, 2)
    def _(g):
        catt[g] = scores(g, 0, own_end)

    outs += [history_block(2)]

    @pl.loop(1, n_user)
    def _(k):
        slot_copy(k).wait_recv()

    for t in range(n_slot):
        e = eslot[:, t * chunk : (t + 1) * chunk].reshape(d, cand)
        e = jnp.transpose(e.astype(F32)).astype(BF16)
        at = pl.ds(own_end + t * cand, cand)
        for g in range(2):
            c = g * gw
            pv = nn(e, win[:, d + c : d + c + gw])
            pk = nn(e, win[:, 3 * d + c : 3 * d + c + gw])
            pre_slot[t, :, c : c + gw] = pv
            pre_slot[t, :, d + c : d + c + gw] = pk
            v2[g, at] = silu(pv).astype(BF16)
            k2[g, at] = silu(pk).astype(BF16)

    n_key = k2.shape[1]

    @pl.loop(0, 2)
    def _(g):
        catt[g] += scores(g, own_end, n_key)

    n0, n1, inv = normalize(catt[0], catt[1])
    uc0 = uc[0].astype(F32)
    uc1 = uc[1].astype(F32)
    gm0 = gmix[:, :gw]
    gm1 = gmix[:, gw:]
    gn0 = gm0 * uc0
    gn1 = gm1 * uc1
    mean_g = (jnp.sum(gn0, 1, keepdims=True) + jnp.sum(gn1, 1, keepdims=True)) / d
    mean_gn = (jnp.sum(gn0 * n0, 1, keepdims=True) + jnp.sum(gn1 * n1, 1, keepdims=True)) / d
    gatt[0] = (inv * (gn0 - mean_g - n0 * mean_gn)).astype(BF16)
    gatt[1] = (inv * (gn1 - mean_g - n1 * mean_gn)).astype(BF16)
    gmix[:, :gw] = gm0 * n0
    gmix[:, gw:] = gm1 * n1
    m0 = (n0 * uc0).astype(BF16)
    m1 = (n1 * uc1).astype(BF16)

    def score_grads(g, lo, hi):
        ga = stacked_heads(gatt[g])
        gs = (nt(ga, v2[g, lo:hi]) * slope[g, :, lo:hi] * scale).astype(BF16)
        late = max(lo, rows)
        gkv[0, g, late - rows : hi - rows] = tn(
            gs[:, late - lo :], stacked_heads(qc[g])) * (2.0 / scale)
        gkv[1, g, late - rows : hi - rows] = tn(wts[g, :, late - rows : hi - rows], ga)
        return unstacked_heads(nn(gs, k2[g, lo:hi]))

    @pl.loop(0, 2)
    def _(g):
        gq[g] = score_grads(g, own_end, n_key)

    for t in range(n_slot):
        at = pl.ds(cand + t * cand, cand)
        total = jnp.zeros((d, cand), F32)
        for g in range(2):
            c = g * gw
            dk = (gkv[0, g, at] * silu_slope(pre_slot[t, :, d + c : d + c + gw])).astype(BF16)
            dv = (gkv[1, g, at] * silu_slope(pre_slot[t, :, c : c + gw])).astype(BF16)
            total = total + nt(win[:, d + c : d + c + gw], dv)
            total = total + nt(win[:, 3 * d + c : 3 * d + c + gw], dk)
        dsend[:, t * chunk : (t + 1) * chunk] = total.astype(BF16).reshape(n_user, chunk, cand)

    drecv[me_u] = dsend[me_u]

    @pl.loop(1, n_user)
    def _(k):
        back_copy(k).start()

    coutv[...] = (nn(m0, wout[:gw]) + nn(m1, wout[gw:]) + own.astype(F32)).astype(BF16)
    cout_copy = pltpu.make_async_copy(coutv, cand_out, out_sem.at[4])
    cout_copy.start()

    @pl.loop(0, 2)
    def _(g):
        gq[g] += score_grads(g, 0, own_end)

    total = jnp.transpose(gcand[...].astype(F32))
    for g in range(2):
        c = g * gw
        for part, grad in (
            (0, gmix[:, c : c + gw]),
            (1, gkv[1, g, :cand]),
            (2, gq[g]),
            (3, gkv[0, g, :cand]),
        ):
            cl = part * d + c
            dp = (grad * silu_slope(pre_own[:, cl : cl + gw])).astype(BF16)
            total = total + nt(win[:, cl : cl + gw], dp)
    share[...] = total.astype(BF16).reshape(share.shape)
    share_in[me_i] = share[me_i]

    @pl.loop(1, n_item)
    def _(k):
        share_copy(k).start()

    outs += [history_block(3)]

    @pl.loop(1, n_user)
    def _(k):
        back_copy(k).wait_recv()

    summed = nn(back[...], drecv[...].reshape(n_user * line, cand)).astype(BF16)
    csum[...] = summed.reshape(csum.shape)

    @pl.loop(0, n_user)
    def _(r):
        @pl.when(not_me((holder, r)))
        def _():
            fin_copy(r).start()

    @pl.when(at_home)
    def _():
        fin[me_u] = csum[me_u]

    outs += [history_block(0)]

    @pl.loop(1, n_item)
    def _(k):
        tagi_copy(k).wait_recv()
        share_copy(k).wait_recv()

    ids_t = jnp.concatenate([tags_i[i, 0:1] for i in range(n_item)], 0)
    ids_t = jnp.transpose(ids_t.astype(F32)).astype(jnp.int32)
    col = lax.broadcasted_iota(jnp.int32, (cand, vb), 1)
    tg = jnp.zeros((piece, vb), F32)
    for i in range(n_item):
        hotc[i] = jnp.where(col == ids_t[:, i : i + 1], 1.0, 0.0).astype(BF16)
        tg = tg + nn(share_in[i], hotc[i])
    tgv[...] = tg

    @pl.loop(0, n_user)
    def _(n):
        @pl.when(not_me((n // per, me_i * per + lax.rem(n, per))))
        def _():
            fin_arrival(n).wait_recv()

    tg = tgv[...]
    for i in range(n_item):
        tg = tg + nn(fin[i * per : (i + 1) * per].reshape(piece, cand), hotc[i])
    tgv[...] = tg
    tg_copy = pltpu.make_async_copy(tgv, tgrad_out, out_sem.at[5])
    tg_copy.start()

    @pl.loop(1, n_item)
    def _(k):
        tagi_copy(k).wait_send()
        share_copy(k).wait_send()

    @pl.loop(1, n_user)
    def _(k):
        tag_copy(k).wait_send()
        own_copy(k).wait_send()
        slot_copy(k).wait_send()
        back_copy(k).wait_send()

    @pl.loop(0, n_user)
    def _(n):
        @pl.when(not_me(worker(n)))
        def _():
            tab_copy(n).wait_send()

        @pl.when(not_me((holder, n)))
        def _():
            fin_copy(n).wait_send()

    for c in outs:
        c.wait()
    cout_copy.wait()
    tg_copy.wait()


def local(history, hist_len, cand_ids, cand_lists, item_table, w_in, w_out, grad_cand):
    rows, d = history.shape[1:]
    cand = cand_ids.shape[1]
    n_slot = cand_lists.shape[1]
    vb, piece = item_table.shape
    n_item = lax.axis_size("item")
    n_user = lax.axis_size("user")
    gw = d // 2
    chunk = d // n_user
    n_late = (1 + n_slot) * cand
    n_key = rows + n_late
    vmem = pl.BlockSpec(memory_space=pltpu.VMEM)
    smem = pl.BlockSpec(memory_space=pltpu.SMEM)
    hbm = pl.BlockSpec(memory_space=pl.ANY)
    V = pltpu.VMEM
    dma = pltpu.SemaphoreType.DMA
    scratch = dict(
        hist=V((rows, d), BF16), win=V((d, 4 * d), BF16), wout=V((d, d), BF16),
        gcand=V((cand, d), BF16),
        tabc=V((n_user, chunk, vb), BF16),
        tags=V((n_user, 8, cand), jnp.int32), tags_i=V((n_item, 8, cand), jnp.int32),
        pick=V((n_user * n_slot * chunk, n_user * chunk), BF16),
        back=V((n_user * chunk, n_user * n_slot * chunk), BF16),
        hotc=V((n_item, cand, vb), BF16),
        e_all=V((n_user, chunk, cand), BF16), disp=V((n_user, n_slot * chunk, cand), BF16),
        eown=V((n_user, chunk, cand), BF16), eslot=V((n_user, n_slot * chunk, cand), BF16),
        u2=V((2, rows, gw), BF16), q2=V((2, rows, gw), BF16),
        k2=V((2, n_key, gw), BF16), v2=V((2, n_key, gw), BF16),
        att=V((2, QB, gw), F32), catt=V((2, cand, gw), F32), outv=V((rows, d), BF16),
        pre_own=V((cand, 4 * d), F32), pre_slot=V((n_slot, cand, 2 * d), F32),
        uc=V((2, cand, gw), BF16), qc=V((2, cand, gw), BF16), gmix=V((cand, d), F32),
        gatt=V((2, cand, gw), BF16),
        wts=V((2, GROUP * cand, n_late), BF16), slope=V((2, GROUP * cand, n_key), F32),
        gq=V((2, cand, gw), F32), gkv=V((2, 2, n_late, gw), F32),
        dsend=V((n_user, n_slot * chunk, cand), BF16),
        drecv=V((n_user, n_slot * chunk, cand), BF16),
        share=V((n_item, piece, cand), BF16), share_in=V((n_item, piece, cand), BF16),
        csum=V((n_user, chunk, cand), BF16), fin=V((n_user, chunk, cand), BF16),
        coutv=V((cand, d), BF16), tgv=V((piece, vb), F32),
        local_sem=dma((5,)), out_sem=dma((6,)),
        s_tab=dma((n_user,)), r_tab=dma((n_user,)),
        s_tag=dma((n_user,)), r_tag=dma((n_user,)),
        s_tagi=dma((n_item,)), r_tagi=dma((n_item,)),
        s_own=dma((n_user,)), r_own=dma((n_user,)),
        s_slot=dma((n_user,)), r_slot=dma((n_user,)),
        s_back=dma((n_user,)), r_back=dma((n_user,)),
        s_share=dma((n_item,)), r_share=dma((n_item,)),
        s_fin=dma((n_user,)), r_fin=dma((n_user,)),
    )
    names = list(scratch)

    def body(*refs):
        kernel(*refs[:11], **dict(zip(names, refs[11:])))

    hist_out, cand_out, tgrad = pl.pallas_call(
        body,
        out_shape=(
            jax.ShapeDtypeStruct((rows, d), BF16),
            jax.ShapeDtypeStruct((cand, d), BF16),
            jax.ShapeDtypeStruct((piece, vb), F32),
        ),
        in_specs=[smem, smem, vmem, hbm, hbm, hbm, hbm, hbm],
        out_specs=(hbm, hbm, hbm),
        scratch_shapes=list(scratch.values()),
        compiler_params=pltpu.CompilerParams(
            collective_id=0, has_side_effects=True, vmem_limit_bytes=58 * 1024 * 1024),
    )(
        hist_len, cand_lists[0], cand_ids, item_table.T, history[0], w_in, w_out, grad_cand[0],
    )
    return hist_out[None], cand_out[None], tgrad.T


def solution(mesh):
    in_specs = (
        P(("item", "user"), None, None),
        P(("item", "user")),
        P(("item", "user"), None),
        P(("item", "user"), None),
        P("user", "item"),
        P(),
        P(),
        P(("item", "user"), None, None),
    )
    out_specs = (
        P(("item", "user"), None, None),
        P(("item", "user"), None, None),
        P("user", "item"),
    )
    return jax.shard_map(local, mesh=mesh, in_specs=in_specs, out_specs=out_specs, check_vma=False)
```

```python
import functools

import jax
import jax.numpy as jnp
from jax import lax
from jax.experimental import pallas as pl
from jax.experimental.pallas import tpu as pltpu
from jax.sharding import PartitionSpec as P

H = 8
GROUP = 4
NORM_EPS = 1e-05
QB = 256
MESH = pl.DeviceIdType.MESH

F32 = jnp.float32
BF16 = jnp.bfloat16


def nn(a, b):
    return lax.dot_general(a, b, (((1,), (0,)), ((), ())), preferred_element_type=F32)


def nt(a, b):
    return lax.dot_general(a, b, (((1,), (1,)), ((), ())), preferred_element_type=F32)


def tn(a, b):
    return lax.dot_general(a, b, (((0,), (0,)), ((), ())), preferred_element_type=F32)


def silu(v):
    half = 0.5 * v
    return half + half * jnp.tanh(half)


def silu_slope(v):
    half = 0.5 * v
    sig = 0.5 + 0.5 * jnp.tanh(half)
    return sig + (v * sig) * (1.0 - sig)


def head_lane(shape, h):
    lane = lax.broadcasted_iota(jnp.int32, shape, len(shape) - 1)
    width = shape[-1] // GROUP
    return (lane >= h * width) & (lane < (h + 1) * width)


def only_head(x, h):
    return jnp.where(head_lane(x.shape, h), x, jnp.zeros_like(x))


def stacked_heads(x):
    return jnp.concatenate([only_head(x, h) for h in range(GROUP)], 0)


def unstacked_heads(x):
    rows = x.shape[0] // GROUP
    total = only_head(x[:rows], 0)
    for h in range(1, GROUP):
        total = total + only_head(x[h * rows : (h + 1) * rows], h)
    return total


def kernel(
    len_hbm, lists_hbm, ids_hbm, table_hbm, hist_hbm, win_hbm, wout_hbm, gcand_hbm,
    hist_out, cand_out, tgrad_out, *,
    len_ref, lists_ref, ids_ref, hist, win, wout, gcand, tabv, hold, tags, tags_i, pick, back, hotc, e_all, disp, eown, eslot,
    u2, q2, k2, v2, att, catt, outv, pre_own, pre_slot, uc, qc, gmix, gatt, wts, slope, gq, gkv,
    dsend, drecv, share, share_in, csum, fin, coutv, tgv,
    local_sem, out_sem, s_tab, r_tab, s_tag, r_tag, s_tagi, r_tagi, s_own, r_own, s_slot, r_slot,
    s_back, r_back, s_share, r_share, s_fin, r_fin,
):
    n_item = lax.axis_size("item")
    n_user = lax.axis_size("user")
    me_i = lax.axis_index("item")
    me_u = lax.axis_index("user")
    rows, d = hist.shape
    cand = gcand.shape[0]
    chunk = hold.shape[1]
    piece, vb = tabv.shape
    per = piece // chunk
    gw = d // 2
    n_slot = eslot.shape[1] // chunk
    own_end = rows + cand
    scale = (d // H) ** (-0.5)
    barrier = pltpu.get_barrier_semaphore()
    def chunk_of(k):
        return lax.rem(k // per + n_item - me_i, n_item) * per + lax.rem(k, per)

    my_chunk = chunk_of(me_u)
    holder = my_chunk // per
    at_home = holder == me_i

    def peer_i(k):
        return {"item": lax.rem(me_i + k, n_item)}

    def peer_u(k):
        return {"user": lax.rem(me_u + k, n_user)}

    def worker(n):
        row = lax.rem(me_i + n // per, n_item)
        return (row, lax.rem(me_i + row, n_item) * per + lax.rem(n, per))

    def not_me(place):
        return jnp.logical_or(place[0] != me_i, place[1] != me_u)

    def signal(place):
        pl.semaphore_signal(barrier, inc=1, device_id=place, device_id_type=MESH)

    for k in range(1, n_item):
        signal(peer_i(k))
    for k in range(1, n_user):
        signal(peer_u(k))
    for n in range(n_user):
        @pl.when(not_me((holder, n)))
        def _():
            signal((holder, n))

    small = [
        pltpu.make_async_copy(len_hbm, len_ref, local_sem.at[0]),
        pltpu.make_async_copy(lists_hbm, lists_ref, local_sem.at[1]),
        pltpu.make_async_copy(ids_hbm, ids_ref, local_sem.at[2]),
        pltpu.make_async_copy(table_hbm, tabv, local_sem.at[3]),
    ]
    copies = [
        pltpu.make_async_copy(hist_hbm, hist, local_sem.at[4]),
        pltpu.make_async_copy(win_hbm, win, local_sem.at[5]),
        pltpu.make_async_copy(gcand_hbm, gcand, local_sem.at[6]),
        pltpu.make_async_copy(wout_hbm, wout, local_sem.at[7]),
    ]
    for c in small + copies:
        c.start()
    for c in small:
        c.wait()
    length = len_ref[0]

    lane = lax.broadcasted_iota(jnp.int32, (1, cand), 1)
    key_row = jnp.zeros((1, cand), jnp.int32)
    for t in range(n_slot):
        key_row = jnp.where(lane // chunk == t, lists_ref[0, t] * chunk + lane - t * chunk, key_row)
    tag = jnp.concatenate([ids_ref[...], key_row, jnp.zeros((6, cand), jnp.int32)], 0)
    tags[me_u] = tag
    tags_i[me_i] = tag

    def remote(src, dst, send, recv, place):
        return pltpu.make_async_remote_copy(
            src_ref=src, dst_ref=dst, send_sem=send, recv_sem=recv, device_id=place,
            device_id_type=MESH)

    def tag_copy(k):
        return remote(tags.at[me_u], tags.at[me_u], s_tag.at[k], r_tag.at[k], peer_u(k))

    def tagi_copy(k):
        return remote(tags_i.at[me_i], tags_i.at[me_i], s_tagi.at[k], r_tagi.at[k], peer_i(k))

    def row_of(n):
        return lax.rem(me_i + n // per, n_item)

    def tab_copy(n):
        return remote(hold.at[row_of(n) * per + n % per], e_all.at[me_u], s_tab.at[n],
                      r_tab.at[me_u], worker(n))

    def tab_arrival(u):
        return remote(e_all.at[u], e_all.at[u], s_tab.at[u], r_tab.at[u], (holder, u))

    def own_copy(k):
        to = lax.rem(me_u + k, n_user)
        return remote(e_all.at[to], eown.at[my_chunk], s_own.at[k], r_own.at[k], peer_u(k))

    def slot_copy(k):
        to = lax.rem(me_u + k, n_user)
        return remote(disp.at[to], eslot.at[my_chunk], s_slot.at[k], r_slot.at[k], peer_u(k))

    def back_copy(k):
        to = lax.rem(me_u + k, n_user)
        return remote(dsend.at[chunk_of(to)], drecv.at[me_u], s_back.at[k], r_back.at[k], peer_u(k))

    def share_copy(k):
        to = lax.rem(me_i + k, n_item)
        return remote(share.at[to], share_in.at[me_i], s_share.at[k], r_share.at[k], peer_i(k))

    def fin_copy(r):
        n = me_i * per + lax.rem(me_u, per)
        return remote(csum.at[r], fin.at[n], s_fin.at[r], r_fin.at[n], (holder, r))

    def fin_from(n):
        row = n // per
        return (row, lax.rem(me_i + row, n_item) * per + lax.rem(n, per))

    def fin_arrival(n):
        return remote(fin.at[n], fin.at[n], s_fin.at[n], r_fin.at[n], fin_from(n))

    pl.semaphore_wait(barrier, n_item + 2 * n_user - 2 - at_home.astype(jnp.int32))

    @pl.loop(1, n_item)
    def _(k):
        tagi_copy(k).start()

    @pl.loop(1, n_user)
    def _(k):
        tag_copy(k).start()

    for c in copies:
        c.wait()

    def project(b):
        at = pl.ds(pl.multiple_of(b * QB, QB), QB)
        x = hist[at]
        keep = (b * QB + lax.broadcasted_iota(jnp.int32, (QB, 1), 0)) < length
        for g in range(2):
            c = g * gw
            u2[g, at] = silu(nn(x, win[:, c : c + gw])).astype(BF16)
            val = silu(nn(x, win[:, d + c : d + c + gw]))
            v2[g, at] = jnp.where(keep, val, 0.0).astype(BF16)
            q2[g, at] = silu(nn(x, win[:, 2 * d + c : 2 * d + c + gw])).astype(BF16) * (scale / 2)
            k2[g, at] = silu(nn(x, win[:, 3 * d + c : 3 * d + c + gw])).astype(BF16)

    half = rows // QB // 2
    pl.loop(0, half)(project)

    @pl.loop(1, n_item)
    def _(k):
        tagi_copy(k).wait_recv()

    for i in range(n_item):
        at = lax.broadcasted_iota(jnp.int32, (vb, cand), 0)
        hot = jnp.where(at == tags_i[i, 0:1], 1.0, 0.0).astype(BF16)
        found = nn(tabv[...], hot).astype(BF16)
        for p in range(per):
            hold[i * per + p] = found[p * chunk : (p + 1) * chunk]

    for n in range(n_user):
        @pl.when(not_me(worker(n)))
        def _():
            tab_copy(n).start()

    @pl.when(at_home)
    def _():
        e_all[me_u] = hold[me_i * per + lax.rem(me_u, per)]

    pl.loop(half, rows // QB)(project)

    gmix[...] = nt(gcand[...], wout[...])

    @pl.loop(1, n_user)
    def _(k):
        tag_copy(k).wait_recv()

    keys = jnp.concatenate([tags[u, 1:2] for u in range(n_user)], 0)
    keys_t = jnp.transpose(keys.astype(F32)).astype(jnp.int32)
    line = n_slot * chunk
    col = lax.broadcasted_iota(jnp.int32, (line, n_user * chunk), 1)
    for u in range(n_user):
        pick[u * line : (u + 1) * line] = jnp.where(
            col == keys_t[:, u : u + 1], 1.0, 0.0).astype(BF16)

    @pl.loop(0, n_user)
    def _(u):
        @pl.when(not_me((holder, u)))
        def _():
            tab_arrival(u).wait_recv()

    eown[my_chunk] = e_all[me_u]

    @pl.loop(1, n_user)
    def _(k):
        own_copy(k).start()

    picked = nn(pick[...], e_all[...].reshape(n_user * chunk, cand)).astype(BF16)
    disp[...] = picked.reshape(disp.shape)
    eslot[my_chunk] = disp[me_u]

    @pl.loop(1, n_user)
    def _(k):
        slot_copy(k).start()

    row = lax.broadcasted_iota(jnp.int32, (n_user * chunk, line), 0)
    for u in range(n_user):
        back[:, u * line : (u + 1) * line] = jnp.where(
            row == tags[u, 1:2], 1.0, 0.0).astype(BF16)

    def normalize(a0, a1):
        mean = (jnp.sum(a0, 1, keepdims=True) + jnp.sum(a1, 1, keepdims=True)) / d
        a0 = a0 - mean
        a1 = a1 - mean
        var = (jnp.sum(a0 * a0, 1, keepdims=True) + jnp.sum(a1 * a1, 1, keepdims=True)) / d
        inv = lax.rsqrt(var + NORM_EPS)
        return a0 * inv, a1 * inv, inv

    def history_block(b):
        lo = b * QB
        n = lo + QB

        @pl.loop(0, 2)
        def _(g):
            q = q2[g, lo:n]
            key = k2[g, :n]
            val = v2[g, :n]
            total = jnp.zeros((QB, gw), F32)
            for h in range(GROUP):
                y = nt(only_head(q, h), key)
                w = y + y * jnp.tanh(y)
                last = w[:, lo:]
                r = lax.broadcasted_iota(jnp.int32, (QB, QB), 0)
                c = lax.broadcasted_iota(jnp.int32, (QB, QB), 1)
                last = jnp.where(c <= r, last, 0.0).astype(BF16)
                if b:
                    w = jnp.concatenate([w[:, :lo].astype(BF16), last], 1)
                else:
                    w = last
                total = total + only_head(nn(w, val), h)
            att[g] = total

        n0, n1, _ = normalize(att[0], att[1])
        m0 = (n0 * u2[0, lo:n].astype(F32)).astype(BF16)
        m1 = (n1 * u2[1, lo:n].astype(F32)).astype(BF16)
        out = nn(m0, wout[:gw]) + nn(m1, wout[gw:]) + hist[lo:n].astype(F32)
        keep = (lo + lax.broadcasted_iota(jnp.int32, (QB, 1), 0)) < length
        outv[lo:n] = jnp.where(keep, out, 0.0).astype(BF16)
        copy = pltpu.make_async_copy(
            outv.at[pl.ds(lo, QB)], hist_out.at[pl.ds(lo, QB)], out_sem.at[b])
        copy.start()
        return copy

    outs = [history_block(1)]

    @pl.loop(1, n_user)
    def _(k):
        own_copy(k).wait_recv()

    own = jnp.transpose(eown[...].reshape(d, cand).astype(F32)).astype(BF16)
    pre_own[...] = nn(own, win[...])
    for g in range(2):
        c = g * gw
        uc[g] = silu(pre_own[:, c : c + gw]).astype(BF16)
        v2[g, rows:own_end] = silu(pre_own[:, d + c : d + c + gw]).astype(BF16)
        qc[g] = silu(pre_own[:, 2 * d + c : 2 * d + c + gw]).astype(BF16) * (scale / 2)
        k2[g, rows:own_end] = silu(pre_own[:, 3 * d + c : 3 * d + c + gw]).astype(BF16)

    def scores(g, lo, hi):
        y = nt(stacked_heads(qc[g]), k2[g, lo:hi])
        t = jnp.tanh(y)
        w = y + y * t
        p = 0.5 + 0.5 * t
        slope[g, :, lo:hi] = p + w * (1.0 - p)
        wb = w.astype(BF16)
        late = max(lo, rows)
        wts[g, :, late - rows : hi - rows] = wb[:, late - lo :]
        return unstacked_heads(nn(wb, v2[g, lo:hi]))

    @pl.loop(0, 2)
    def _(g):
        catt[g] = scores(g, 0, own_end)

    outs += [history_block(2)]

    @pl.loop(1, n_user)
    def _(k):
        slot_copy(k).wait_recv()

    for t in range(n_slot):
        e = eslot[:, t * chunk : (t + 1) * chunk].reshape(d, cand)
        e = jnp.transpose(e.astype(F32)).astype(BF16)
        at = pl.ds(own_end + t * cand, cand)
        for g in range(2):
            c = g * gw
            pv = nn(e, win[:, d + c : d + c + gw])
            pk = nn(e, win[:, 3 * d + c : 3 * d + c + gw])
            pre_slot[t, :, c : c + gw] = pv
            pre_slot[t, :, d + c : d + c + gw] = pk
            v2[g, at] = silu(pv).astype(BF16)
            k2[g, at] = silu(pk).astype(BF16)

    n_key = k2.shape[1]

    @pl.loop(0, 2)
    def _(g):
        catt[g] += scores(g, own_end, n_key)

    n0, n1, inv = normalize(catt[0], catt[1])
    uc0 = uc[0].astype(F32)
    uc1 = uc[1].astype(F32)
    gm0 = gmix[:, :gw]
    gm1 = gmix[:, gw:]
    gn0 = gm0 * uc0
    gn1 = gm1 * uc1
    mean_g = (jnp.sum(gn0, 1, keepdims=True) + jnp.sum(gn1, 1, keepdims=True)) / d
    mean_gn = (jnp.sum(gn0 * n0, 1, keepdims=True) + jnp.sum(gn1 * n1, 1, keepdims=True)) / d
    gatt[0] = (inv * (gn0 - mean_g - n0 * mean_gn)).astype(BF16)
    gatt[1] = (inv * (gn1 - mean_g - n1 * mean_gn)).astype(BF16)
    gmix[:, :gw] = gm0 * n0
    gmix[:, gw:] = gm1 * n1
    m0 = (n0 * uc0).astype(BF16)
    m1 = (n1 * uc1).astype(BF16)

    def score_grads(g, lo, hi):
        ga = stacked_heads(gatt[g])
        gs = (nt(ga, v2[g, lo:hi]) * slope[g, :, lo:hi] * scale).astype(BF16)
        late = max(lo, rows)
        gkv[0, g, late - rows : hi - rows] = tn(
            gs[:, late - lo :], stacked_heads(qc[g])) * (2.0 / scale)
        gkv[1, g, late - rows : hi - rows] = tn(wts[g, :, late - rows : hi - rows], ga)
        return unstacked_heads(nn(gs, k2[g, lo:hi]))

    @pl.loop(0, 2)
    def _(g):
        gq[g] = score_grads(g, own_end, n_key)

    for t in range(n_slot):
        at = pl.ds(cand + t * cand, cand)
        total = jnp.zeros((d, cand), F32)
        for g in range(2):
            c = g * gw
            dk = (gkv[0, g, at] * silu_slope(pre_slot[t, :, d + c : d + c + gw])).astype(BF16)
            dv = (gkv[1, g, at] * silu_slope(pre_slot[t, :, c : c + gw])).astype(BF16)
            total = total + nt(win[:, d + c : d + c + gw], dv)
            total = total + nt(win[:, 3 * d + c : 3 * d + c + gw], dk)
        dsend[:, t * chunk : (t + 1) * chunk] = total.astype(BF16).reshape(n_user, chunk, cand)

    drecv[me_u] = dsend[my_chunk]

    @pl.loop(1, n_user)
    def _(k):
        back_copy(k).start()

    coutv[...] = (nn(m0, wout[:gw]) + nn(m1, wout[gw:]) + own.astype(F32)).astype(BF16)
    cout_copy = pltpu.make_async_copy(coutv, cand_out, out_sem.at[4])
    cout_copy.start()

    @pl.loop(0, 2)
    def _(g):
        gq[g] += score_grads(g, 0, own_end)

    total = jnp.transpose(gcand[...].astype(F32))
    for g in range(2):
        c = g * gw
        for part, grad in (
            (0, gmix[:, c : c + gw]),
            (1, gkv[1, g, :cand]),
            (2, gq[g]),
            (3, gkv[0, g, :cand]),
        ):
            cl = part * d + c
            dp = (grad * silu_slope(pre_own[:, cl : cl + gw])).astype(BF16)
            total = total + nt(win[:, cl : cl + gw], dp)
    share[...] = total.astype(BF16).reshape(share.shape)
    share_in[me_i] = share[me_i]

    @pl.loop(1, n_item)
    def _(k):
        share_copy(k).start()

    outs += [history_block(3)]

    @pl.loop(1, n_user)
    def _(k):
        back_copy(k).wait_recv()

    summed = nn(back[...], drecv[...].reshape(n_user * line, cand)).astype(BF16)
    csum[...] = summed.reshape(csum.shape)

    @pl.loop(0, n_user)
    def _(r):
        @pl.when(not_me((holder, r)))
        def _():
            fin_copy(r).start()

    @pl.when(at_home)
    def _():
        fin[me_i * per + lax.rem(me_u, per)] = csum[me_u]

    outs += [history_block(0)]

    @pl.loop(1, n_item)
    def _(k):
        share_copy(k).wait_recv()

    ids_t = jnp.concatenate([tags_i[i, 0:1] for i in range(n_item)], 0)
    ids_t = jnp.transpose(ids_t.astype(F32)).astype(jnp.int32)
    col = lax.broadcasted_iota(jnp.int32, (cand, vb), 1)
    tg = jnp.zeros((piece, vb), F32)
    for i in range(n_item):
        hotc[i] = jnp.where(col == ids_t[:, i : i + 1], 1.0, 0.0).astype(BF16)
        tg = tg + nn(share_in[i], hotc[i])
    tgv[...] = tg

    @pl.loop(0, n_user)
    def _(n):
        @pl.when(not_me(fin_from(n)))
        def _():
            fin_arrival(n).wait_recv()

    tg = tgv[...]
    for i in range(n_item):
        tg = tg + nn(fin[i * per : (i + 1) * per].reshape(piece, cand), hotc[i])
    tgv[...] = tg
    tg_copy = pltpu.make_async_copy(tgv, tgrad_out, out_sem.at[5])
    tg_copy.start()

    @pl.loop(1, n_item)
    def _(k):
        tagi_copy(k).wait_send()
        share_copy(k).wait_send()

    @pl.loop(1, n_user)
    def _(k):
        tag_copy(k).wait_send()
        own_copy(k).wait_send()
        slot_copy(k).wait_send()
        back_copy(k).wait_send()

    @pl.loop(0, n_user)
    def _(n):
        @pl.when(not_me(worker(n)))
        def _():
            tab_copy(n).wait_send()

        @pl.when(not_me((holder, n)))
        def _():
            fin_copy(n).wait_send()

    for c in outs:
        c.wait()
    cout_copy.wait()
    tg_copy.wait()


PARTS = 8


def hand_over_kernel(a, b, c, a_out, b_out, c_out, a_v, b_v, c_v, sem_in, sem_out):
    n = a.shape[0] // PARTS
    steps = []
    for j in range(PARTS):
        at = pl.ds(j * n, n)
        steps.append((a.at[at], a_v.at[at], a_out.at[at]))
    steps += [(b, b_v, b_out), (c, c_v, c_out)]
    loads = [pltpu.make_async_copy(x, v, sem_in.at[j]) for j, (x, v, _) in enumerate(steps)]
    stores = [pltpu.make_async_copy(v, y, sem_out.at[j]) for j, (_, v, y) in enumerate(steps)]
    for m in loads:
        m.start()
    for m, w in zip(loads, stores):
        m.wait()
        w.start()
    for w in stores:
        w.wait()


def hand_over(*arrays):
    hbm = pl.BlockSpec(memory_space=pl.ANY)
    return pl.pallas_call(
        hand_over_kernel,
        out_shape=tuple(jax.ShapeDtypeStruct(x.shape, x.dtype) for x in arrays),
        in_specs=[hbm] * 3,
        out_specs=(hbm,) * 3,
        scratch_shapes=[pltpu.VMEM(x.shape, x.dtype) for x in arrays]
        + [pltpu.SemaphoreType.DMA((PARTS + 2,))] * 2,
    )(*arrays)


def local(history, hist_len, cand_ids, cand_lists, item_table, w_in, w_out, grad_cand):
    rows, d = history.shape[1:]
    cand = cand_ids.shape[1]
    n_slot = cand_lists.shape[1]
    vb, piece = item_table.shape
    n_item = lax.axis_size("item")
    n_user = lax.axis_size("user")
    gw = d // 2
    chunk = d // n_user
    n_late = (1 + n_slot) * cand
    n_key = rows + n_late
    hbm = pl.BlockSpec(memory_space=pl.ANY)
    V = pltpu.VMEM
    dma = pltpu.SemaphoreType.DMA
    scratch = dict(
        len_ref=pltpu.SMEM((1,), jnp.int32), lists_ref=pltpu.SMEM((1, n_slot), jnp.int32),
        ids_ref=V((1, cand), jnp.int32),
        hist=V((rows, d), BF16), win=V((d, 4 * d), BF16), wout=V((d, d), BF16),
        gcand=V((cand, d), BF16),
        tabv=V((piece, vb), BF16), hold=V((n_user, chunk, cand), BF16),
        tags=V((n_user, 8, cand), jnp.int32), tags_i=V((n_item, 8, cand), jnp.int32),
        pick=V((n_user * n_slot * chunk, n_user * chunk), BF16),
        back=V((n_user * chunk, n_user * n_slot * chunk), BF16),
        hotc=V((n_item, cand, vb), BF16),
        e_all=V((n_user, chunk, cand), BF16), disp=V((n_user, n_slot * chunk, cand), BF16),
        eown=V((n_user, chunk, cand), BF16), eslot=V((n_user, n_slot * chunk, cand), BF16),
        u2=V((2, rows, gw), BF16), q2=V((2, rows, gw), BF16),
        k2=V((2, n_key, gw), BF16), v2=V((2, n_key, gw), BF16),
        att=V((2, QB, gw), F32), catt=V((2, cand, gw), F32), outv=V((rows, d), BF16),
        pre_own=V((cand, 4 * d), F32), pre_slot=V((n_slot, cand, 2 * d), F32),
        uc=V((2, cand, gw), BF16), qc=V((2, cand, gw), BF16), gmix=V((cand, d), F32),
        gatt=V((2, cand, gw), BF16),
        wts=V((2, GROUP * cand, n_late), BF16), slope=V((2, GROUP * cand, n_key), F32),
        gq=V((2, cand, gw), F32), gkv=V((2, 2, n_late, gw), F32),
        dsend=V((n_user, n_slot * chunk, cand), BF16),
        drecv=V((n_user, n_slot * chunk, cand), BF16),
        share=V((n_item, piece, cand), BF16), share_in=V((n_item, piece, cand), BF16),
        csum=V((n_user, chunk, cand), BF16), fin=V((n_user, chunk, cand), BF16),
        coutv=V((cand, d), BF16), tgv=V((piece, vb), F32),
        local_sem=dma((8,)), out_sem=dma((6,)),
        s_tab=dma((n_user,)), r_tab=dma((n_user,)),
        s_tag=dma((n_user,)), r_tag=dma((n_user,)),
        s_tagi=dma((n_item,)), r_tagi=dma((n_item,)),
        s_own=dma((n_user,)), r_own=dma((n_user,)),
        s_slot=dma((n_user,)), r_slot=dma((n_user,)),
        s_back=dma((n_user,)), r_back=dma((n_user,)),
        s_share=dma((n_item,)), r_share=dma((n_item,)),
        s_fin=dma((n_user,)), r_fin=dma((n_user,)),
    )
    names = list(scratch)

    def body(*refs):
        kernel(*refs[:11], **dict(zip(names, refs[11:])))

    hist_out, cand_out, tgrad = pl.pallas_call(
        body,
        out_shape=(
            jax.ShapeDtypeStruct((rows, d), BF16),
            jax.ShapeDtypeStruct((cand, d), BF16),
            jax.ShapeDtypeStruct((piece, vb), F32),
        ),
        in_specs=[hbm] * 8,
        out_specs=(hbm, hbm, hbm),
        scratch_shapes=list(scratch.values()),
        compiler_params=pltpu.CompilerParams(
            collective_id=0, has_side_effects=True, vmem_limit_bytes=58 * 1024 * 1024),
    )(
        hist_len, cand_lists, cand_ids, item_table.T, history[0], w_in, w_out, grad_cand[0],
    )
    hist_out, cand_out, tgrad = hand_over(hist_out, cand_out, tgrad)
    return hist_out[None], cand_out[None], tgrad.T


def solution(mesh):
    in_specs = (
        P(("item", "user"), None, None),
        P(("item", "user")),
        P(("item", "user"), None),
        P(("item", "user"), None),
        P("user", "item"),
        P(),
        P(),
        P(("item", "user"), None, None),
    )
    out_specs = (
        P(("item", "user"), None, None),
        P(("item", "user"), None, None),
        P("user", "item"),
    )
    return jax.shard_map(local, mesh=mesh, in_specs=in_specs, out_specs=out_specs, check_vma=False)
```

```python
import functools

import jax
import jax.numpy as jnp
from jax import lax
from jax.experimental import pallas as pl
from jax.experimental.pallas import tpu as pltpu
from jax.sharding import PartitionSpec as P

H = 8
GROUP = 4
NORM_EPS = 1e-05
QB = 256
MESH = pl.DeviceIdType.MESH

F32 = jnp.float32
BF16 = jnp.bfloat16


def nn(a, b):
    return lax.dot_general(a, b, (((1,), (0,)), ((), ())), preferred_element_type=F32)


def nt(a, b):
    return lax.dot_general(a, b, (((1,), (1,)), ((), ())), preferred_element_type=F32)


def tn(a, b):
    return lax.dot_general(a, b, (((0,), (0,)), ((), ())), preferred_element_type=F32)


def silu(v):
    half = 0.5 * v
    return half + half * jnp.tanh(half)


def silu_slope(v):
    half = 0.5 * v
    sig = 0.5 + 0.5 * jnp.tanh(half)
    return sig + (v * sig) * (1.0 - sig)


def head_lane(shape, h):
    lane = lax.broadcasted_iota(jnp.int32, shape, len(shape) - 1)
    width = shape[-1] // GROUP
    return (lane >= h * width) & (lane < (h + 1) * width)


def only_head(x, h):
    return jnp.where(head_lane(x.shape, h), x, jnp.zeros_like(x))


def stacked_heads(x):
    return jnp.concatenate([only_head(x, h) for h in range(GROUP)], 0)


def unstacked_heads(x):
    rows = x.shape[0] // GROUP
    total = only_head(x[:rows], 0)
    for h in range(1, GROUP):
        total = total + only_head(x[h * rows : (h + 1) * rows], h)
    return total


def kernel(
    len_hbm, lists_hbm, ids_hbm, table_hbm, hist_hbm, win_hbm, wout_hbm, gcand_hbm,
    hist_out, cand_out, tgrad_out, *,
    len_ref, lists_ref, ids_ref, hist, win, wout, gcand, tabv, hold, tags, tags_i, pick, back, hotc, e_all, disp, eown, eslot,
    u2, q2, k2, v2, att, catt, pre_own, pre_slot, uc, qc, gmix, gatt, wts, slope, gq, gkv,
    dsend, drecv, share, share_in, csum, fin, tgv,
    local_sem, s_tab, r_tab, s_tag, r_tag, s_tagi, r_tagi, s_own, r_own, s_slot, r_slot,
    s_back, r_back, s_share, r_share, s_fin, r_fin,
):
    n_item = lax.axis_size("item")
    n_user = lax.axis_size("user")
    me_i = lax.axis_index("item")
    me_u = lax.axis_index("user")
    rows, d = hist.shape
    cand = gcand.shape[0]
    chunk = e_all.shape[1]
    piece, vb = tabv.shape
    per = piece // chunk
    gw = d // 2
    n_slot = eslot.shape[1] // chunk
    own_end = rows + cand
    scale = (d // H) ** (-0.5)
    barrier = pltpu.get_barrier_semaphore()
    def chunk_of(k):
        return lax.rem(k // per + n_item - me_i, n_item) * per + lax.rem(k, per)

    my_chunk = chunk_of(me_u)
    holder = my_chunk // per
    at_home = holder == me_i

    def peer_i(k):
        return {"item": lax.rem(me_i + k, n_item)}

    def peer_u(k):
        return {"user": lax.rem(me_u + k, n_user)}

    def worker(n):
        row = lax.rem(me_i + n // per, n_item)
        return (row, lax.rem(me_i + row, n_item) * per + lax.rem(n, per))

    def not_me(place):
        return jnp.logical_or(place[0] != me_i, place[1] != me_u)

    def signal(place):
        pl.semaphore_signal(barrier, inc=1, device_id=place, device_id_type=MESH)

    for k in range(1, n_item):
        signal(peer_i(k))
    for k in range(1, n_user):
        signal(peer_u(k))

    small = [
        pltpu.make_async_copy(len_hbm, len_ref, local_sem.at[0]),
        pltpu.make_async_copy(lists_hbm, lists_ref, local_sem.at[1]),
        pltpu.make_async_copy(ids_hbm, ids_ref, local_sem.at[2]),
        pltpu.make_async_copy(table_hbm, tabv, local_sem.at[3]),
    ]
    copies = [
        pltpu.make_async_copy(hist_hbm, hist, local_sem.at[4]),
        pltpu.make_async_copy(win_hbm, win, local_sem.at[5]),
        pltpu.make_async_copy(gcand_hbm, gcand, local_sem.at[6]),
        pltpu.make_async_copy(wout_hbm, wout, local_sem.at[7]),
    ]
    for c in small + copies:
        c.start()

    def build_tags():
        lane = lax.broadcasted_iota(jnp.int32, (1, cand), 1)
        key_row = jnp.zeros((1, cand), jnp.int32)
        for t in range(n_slot):
            key_row = jnp.where(lane // chunk == t, lists_ref[0, t] * chunk + lane - t * chunk, key_row)
        tag = jnp.concatenate([ids_ref[...], key_row, jnp.zeros((6, cand), jnp.int32)], 0)
        tags[me_u] = tag
        tags_i[me_i] = ids_ref[...]

    def remote(src, dst, send, recv, place):
        return pltpu.make_async_remote_copy(
            src_ref=src, dst_ref=dst, send_sem=send, recv_sem=recv, device_id=place,
            device_id_type=MESH)

    def tag_copy(k):
        return remote(tags.at[me_u], tags.at[me_u], s_tag.at[k], r_tag.at[k], peer_u(k))

    def tagi_copy(k):
        return remote(ids_hbm, tags_i.at[me_i], s_tagi.at[k], r_tagi.at[k], peer_i(k))

    def row_of(n):
        return lax.rem(me_i + n // per, n_item)

    def tab_copy(n):
        part = pl.ds((n % per) * chunk, chunk)
        return remote(hold.at[row_of(n), part], e_all.at[me_u], s_tab.at[n], r_tab.at[me_u],
                      worker(n))

    def tab_arrival(u):
        return remote(e_all.at[u], e_all.at[u], s_tab.at[u], r_tab.at[u], (holder, u))

    def own_copy(k):
        to = lax.rem(me_i + k, n_item)
        return remote(hold.at[to], eown.at[me_i], s_own.at[k], r_own.at[k], peer_i(k))

    def slot_copy(k):
        to = lax.rem(me_u + k, n_user)
        return remote(disp.at[to], eslot.at[my_chunk], s_slot.at[k], r_slot.at[k], peer_u(k))

    def back_copy(k):
        to = lax.rem(me_u + k, n_user)
        return remote(dsend.at[chunk_of(to)], drecv.at[me_u], s_back.at[k], r_back.at[k], peer_u(k))

    def share_copy(k):
        to = lax.rem(me_i + k, n_item)
        return remote(share.at[to], share_in.at[me_i], s_share.at[k], r_share.at[k], peer_i(k))

    def fin_copy(r):
        n = me_i * per + lax.rem(me_u, per)
        return remote(csum.at[r], fin.at[n], s_fin.at[r], r_fin.at[n], (holder, r))

    def fin_from(n):
        row = n // per
        return (row, lax.rem(me_i + row, n_item) * per + lax.rem(n, per))

    def fin_arrival(n):
        return remote(fin.at[n], fin.at[n], s_fin.at[n], r_fin.at[n], fin_from(n))

    pl.semaphore_wait(barrier, n_item + n_user - 2)

    @pl.loop(1, n_item)
    def _(k):
        tagi_copy(k).start()

    for c in small:
        c.wait()
    length = len_ref[0]
    build_tags()

    @pl.loop(1, n_user)
    def _(k):
        tag_copy(k).start()

    for c in copies:
        c.wait()

    def normalize(a0, a1):
        mean = (jnp.sum(a0, 1, keepdims=True) + jnp.sum(a1, 1, keepdims=True)) / d
        a0 = a0 - mean
        a1 = a1 - mean
        var = (jnp.sum(a0 * a0, 1, keepdims=True) + jnp.sum(a1 * a1, 1, keepdims=True)) / d
        inv = lax.rsqrt(var + NORM_EPS)
        return a0 * inv, a1 * inv, inv

    def history_block(b):
        lo = b * QB
        n = lo + QB

        @pl.loop(0, 2)
        def _(g):
            q = q2[g, lo:n]
            key = k2[g, :n]
            val = v2[g, :n]
            total = jnp.zeros((QB, gw), F32)
            for h in range(GROUP):
                y = nt(only_head(q, h), key)
                w = y + y * jnp.tanh(y)
                last = w[:, lo:]
                r = lax.broadcasted_iota(jnp.int32, (QB, QB), 0)
                c = lax.broadcasted_iota(jnp.int32, (QB, QB), 1)
                last = jnp.where(c <= r, last, 0.0).astype(BF16)
                if b:
                    w = jnp.concatenate([w[:, :lo].astype(BF16), last], 1)
                else:
                    w = last
                total = total + only_head(nn(w, val), h)
            att[g] = total

        n0, n1, _ = normalize(att[0], att[1])
        m0 = (n0 * u2[0, lo:n].astype(F32)).astype(BF16)
        m1 = (n1 * u2[1, lo:n].astype(F32)).astype(BF16)
        out = nn(m0, wout[:gw]) + nn(m1, wout[gw:]) + hist[lo:n].astype(F32)
        keep = (lo + lax.broadcasted_iota(jnp.int32, (QB, 1), 0)) < length
        hist_out[lo:n] = jnp.where(keep, out, 0.0).astype(BF16)

    def project(b):
        at = pl.ds(pl.multiple_of(b * QB, QB), QB)
        x = hist[at]
        keep = (b * QB + lax.broadcasted_iota(jnp.int32, (QB, 1), 0)) < length
        for g in range(2):
            c = g * gw
            u2[g, at] = silu(nn(x, win[:, c : c + gw])).astype(BF16)
            val = silu(nn(x, win[:, d + c : d + c + gw]))
            v2[g, at] = jnp.where(keep, val, 0.0).astype(BF16)
            q2[g, at] = silu(nn(x, win[:, 2 * d + c : 2 * d + c + gw])).astype(BF16) * (scale / 2)
            k2[g, at] = silu(nn(x, win[:, 3 * d + c : 3 * d + c + gw])).astype(BF16)

    half = rows // QB // 2
    pl.loop(0, half)(project)

    at = lax.broadcasted_iota(jnp.int32, (vb, cand), 0)
    for j in range(n_item):
        i = lax.rem(me_i + j, n_item)
        if j:
            tagi_copy(n_item - j).wait_recv()
        hot = jnp.where(at == tags_i[i], 1.0, 0.0).astype(BF16)
        hold[i] = nn(tabv[...], hot).astype(BF16)
        for n in range(j * per, (j + 1) * per):
            @pl.when(not_me(worker(n)))
            def _():
                tab_copy(n).start()
        if j:
            own_copy(j).start()

    @pl.when(at_home)
    def _():
        part = pl.ds(pl.multiple_of(lax.rem(me_u, per) * chunk, chunk), chunk)
        e_all[me_u] = hold[me_i, part]

    eown[me_i] = hold[me_i]
    pl.loop(half, rows // QB)(project)

    @pl.loop(1, n_user)
    def _(k):
        tag_copy(k).wait_recv()

    keys = jnp.concatenate([tags[u, 1:2] for u in range(n_user)], 0)
    keys_t = jnp.transpose(keys.astype(F32)).astype(jnp.int32)
    line = n_slot * chunk
    col = lax.broadcasted_iota(jnp.int32, (line, n_user * chunk), 1)
    for u in range(n_user):
        pick[u * line : (u + 1) * line] = jnp.where(
            col == keys_t[:, u : u + 1], 1.0, 0.0).astype(BF16)

    history_block(0)

    @pl.loop(0, n_user)
    def _(u):
        @pl.when(not_me((holder, u)))
        def _():
            tab_arrival(u).wait_recv()

    picked = nn(pick[...], e_all[...].reshape(n_user * chunk, cand)).astype(BF16)
    disp[...] = picked.reshape(disp.shape)
    eslot[my_chunk] = disp[me_u]

    @pl.loop(1, n_user)
    def _(k):
        slot_copy(k).start()

    row = lax.broadcasted_iota(jnp.int32, (n_user * chunk, line), 0)
    for u in range(n_user):
        back[:, u * line : (u + 1) * line] = jnp.where(
            row == tags[u, 1:2], 1.0, 0.0).astype(BF16)

    @pl.loop(1, n_item)
    def _(k):
        own_copy(k).wait_recv()

    own = jnp.transpose(eown[...].reshape(d, cand).astype(F32)).astype(BF16)
    pre_own[...] = nn(own, win[...])
    for g in range(2):
        c = g * gw
        uc[g] = silu(pre_own[:, c : c + gw]).astype(BF16)
        v2[g, rows:own_end] = silu(pre_own[:, d + c : d + c + gw]).astype(BF16)
        qc[g] = silu(pre_own[:, 2 * d + c : 2 * d + c + gw]).astype(BF16) * (scale / 2)
        k2[g, rows:own_end] = silu(pre_own[:, 3 * d + c : 3 * d + c + gw]).astype(BF16)

    def scores(g, lo, hi):
        y = nt(stacked_heads(qc[g]), k2[g, lo:hi])
        t = jnp.tanh(y)
        w = y + y * t
        p = 0.5 + 0.5 * t
        slope[g, :, lo:hi] = p + w * (1.0 - p)
        wb = w.astype(BF16)
        late = max(lo, rows)
        wts[g, :, late - rows : hi - rows] = wb[:, late - lo :]
        return unstacked_heads(nn(wb, v2[g, lo:hi]))

    @pl.loop(0, 2)
    def _(g):
        catt[g] = scores(g, 0, own_end)

    history_block(1)
    history_block(2)
    gmix[...] = nt(gcand[...], wout[...])

    @pl.loop(1, n_user)
    def _(k):
        slot_copy(k).wait_recv()

    for t in range(n_slot):
        e = eslot[:, t * chunk : (t + 1) * chunk].reshape(d, cand)
        e = jnp.transpose(e.astype(F32)).astype(BF16)
        at = pl.ds(own_end + t * cand, cand)
        for g in range(2):
            c = g * gw
            pv = nn(e, win[:, d + c : d + c + gw])
            pk = nn(e, win[:, 3 * d + c : 3 * d + c + gw])
            pre_slot[t, :, c : c + gw] = pv
            pre_slot[t, :, d + c : d + c + gw] = pk
            v2[g, at] = silu(pv).astype(BF16)
            k2[g, at] = silu(pk).astype(BF16)

    n_key = k2.shape[1]

    @pl.loop(0, 2)
    def _(g):
        catt[g] += scores(g, own_end, n_key)

    n0, n1, inv = normalize(catt[0], catt[1])
    uc0 = uc[0].astype(F32)
    uc1 = uc[1].astype(F32)
    gm0 = gmix[:, :gw]
    gm1 = gmix[:, gw:]
    gn0 = gm0 * uc0
    gn1 = gm1 * uc1
    mean_g = (jnp.sum(gn0, 1, keepdims=True) + jnp.sum(gn1, 1, keepdims=True)) / d
    mean_gn = (jnp.sum(gn0 * n0, 1, keepdims=True) + jnp.sum(gn1 * n1, 1, keepdims=True)) / d
    gatt[0] = (inv * (gn0 - mean_g - n0 * mean_gn)).astype(BF16)
    gatt[1] = (inv * (gn1 - mean_g - n1 * mean_gn)).astype(BF16)
    gmix[:, :gw] = gm0 * n0
    gmix[:, gw:] = gm1 * n1
    m0 = (n0 * uc0).astype(BF16)
    m1 = (n1 * uc1).astype(BF16)

    def score_grads(g, lo, hi):
        ga = stacked_heads(gatt[g])
        gs = (nt(ga, v2[g, lo:hi]) * slope[g, :, lo:hi] * scale).astype(BF16)
        late = max(lo, rows)
        gkv[0, g, late - rows : hi - rows] = tn(
            gs[:, late - lo :], stacked_heads(qc[g])) * (2.0 / scale)
        gkv[1, g, late - rows : hi - rows] = tn(wts[g, :, late - rows : hi - rows], ga)
        return unstacked_heads(nn(gs, k2[g, lo:hi]))

    @pl.loop(0, 2)
    def _(g):
        gq[g] = score_grads(g, own_end, n_key)

    for t in range(n_slot):
        at = pl.ds(cand + t * cand, cand)
        total = jnp.zeros((d, cand), F32)
        for g in range(2):
            c = g * gw
            dk = (gkv[0, g, at] * silu_slope(pre_slot[t, :, d + c : d + c + gw])).astype(BF16)
            dv = (gkv[1, g, at] * silu_slope(pre_slot[t, :, c : c + gw])).astype(BF16)
            total = total + nt(win[:, d + c : d + c + gw], dv)
            total = total + nt(win[:, 3 * d + c : 3 * d + c + gw], dk)
        dsend[:, t * chunk : (t + 1) * chunk] = total.astype(BF16).reshape(n_user, chunk, cand)

    drecv[me_u] = dsend[my_chunk]

    @pl.loop(1, n_user)
    def _(k):
        back_copy(k).start()

    cand_out[...] = (nn(m0, wout[:gw]) + nn(m1, wout[gw:]) + own.astype(F32)).astype(BF16)

    @pl.loop(0, 2)
    def _(g):
        gq[g] += score_grads(g, 0, own_end)

    total = jnp.transpose(gcand[...].astype(F32))
    for g in range(2):
        c = g * gw
        for part, grad in (
            (0, gmix[:, c : c + gw]),
            (1, gkv[1, g, :cand]),
            (2, gq[g]),
            (3, gkv[0, g, :cand]),
        ):
            cl = part * d + c
            dp = (grad * silu_slope(pre_own[:, cl : cl + gw])).astype(BF16)
            total = total + nt(win[:, cl : cl + gw], dp)
    share[...] = total.astype(BF16).reshape(share.shape)
    share_in[me_i] = share[me_i]

    @pl.loop(1, n_item)
    def _(k):
        share_copy(k).start()

    history_block(3)

    @pl.loop(1, n_user)
    def _(k):
        back_copy(k).wait_recv()

    summed = nn(back[...], drecv[...].reshape(n_user * line, cand)).astype(BF16)
    csum[...] = summed.reshape(csum.shape)

    @pl.loop(0, n_user)
    def _(r):
        @pl.when(not_me((holder, r)))
        def _():
            fin_copy(r).start()

    @pl.when(at_home)
    def _():
        fin[me_i * per + lax.rem(me_u, per)] = csum[me_u]

    @pl.loop(1, n_item)
    def _(k):
        share_copy(k).wait_recv()

    ids_t = jnp.concatenate([tags_i[i] for i in range(n_item)], 0)
    ids_t = jnp.transpose(ids_t.astype(F32)).astype(jnp.int32)
    col = lax.broadcasted_iota(jnp.int32, (cand, vb), 1)
    for i in range(n_item):
        hotc[i] = jnp.where(col == ids_t[:, i : i + 1], 1.0, 0.0).astype(BF16)
    hot_all = hotc[...].reshape(n_item * cand, vb)
    tgv[...] = nn(jnp.concatenate([share_in[i] for i in range(n_item)], 1), hot_all)

    @pl.loop(0, n_user)
    def _(n):
        @pl.when(not_me(fin_from(n)))
        def _():
            fin_arrival(n).wait_recv()

    terms = [fin[i * per : (i + 1) * per].reshape(piece, cand) for i in range(n_item)]
    tgrad_out[...] = tgv[...] + nn(jnp.concatenate(terms, 1), hot_all)

    @pl.loop(1, n_item)
    def _(k):
        tagi_copy(k).wait_send()
        own_copy(k).wait_send()
        share_copy(k).wait_send()

    @pl.loop(1, n_user)
    def _(k):
        tag_copy(k).wait_send()
        slot_copy(k).wait_send()
        back_copy(k).wait_send()

    @pl.loop(0, n_user)
    def _(n):
        @pl.when(not_me(worker(n)))
        def _():
            tab_copy(n).wait_send()

        @pl.when(not_me((holder, n)))
        def _():
            fin_copy(n).wait_send()


def hand_over_kernel(a, b, c, a_out, b_out, c_out, sem):
    moves = [
        pltpu.make_async_copy(x, y, sem.at[j])
        for j, (x, y) in enumerate(((a, a_out), (b, b_out), (c, c_out)))
    ]
    for m in moves:
        m.start()
    for m in moves:
        m.wait()


def hand_over(*arrays):
    hbm = pl.BlockSpec(memory_space=pl.ANY)
    return pl.pallas_call(
        hand_over_kernel,
        out_shape=tuple(jax.ShapeDtypeStruct(x.shape, x.dtype) for x in arrays),
        in_specs=[hbm] * 3,
        out_specs=(hbm,) * 3,
        scratch_shapes=[pltpu.SemaphoreType.DMA((3,))],
        compiler_params=pltpu.CompilerParams(vmem_limit_bytes=1024 * 1024),
    )(*arrays)


def local(history, hist_len, cand_ids, cand_lists, item_table, w_in, w_out, grad_cand):
    rows, d = history.shape[1:]
    cand = cand_ids.shape[1]
    n_slot = cand_lists.shape[1]
    vb, piece = item_table.shape
    n_item = lax.axis_size("item")
    n_user = lax.axis_size("user")
    gw = d // 2
    chunk = d // n_user
    n_late = (1 + n_slot) * cand
    n_key = rows + n_late
    hbm = pl.BlockSpec(memory_space=pl.ANY)
    V = pltpu.VMEM
    dma = pltpu.SemaphoreType.DMA
    scratch = dict(
        len_ref=pltpu.SMEM((1,), jnp.int32), lists_ref=pltpu.SMEM((1, n_slot), jnp.int32),
        ids_ref=V((1, cand), jnp.int32),
        hist=V((rows, d), BF16), win=V((d, 4 * d), BF16), wout=V((d, d), BF16),
        gcand=V((cand, d), BF16),
        tabv=V((piece, vb), BF16), hold=V((n_item, piece, cand), BF16),
        tags=V((n_user, 8, cand), jnp.int32), tags_i=V((n_item, 1, cand), jnp.int32),
        pick=V((n_user * n_slot * chunk, n_user * chunk), BF16),
        back=V((n_user * chunk, n_user * n_slot * chunk), BF16),
        hotc=V((n_item, cand, vb), BF16),
        e_all=V((n_user, chunk, cand), BF16), disp=V((n_user, n_slot * chunk, cand), BF16),
        eown=V((n_item, piece, cand), BF16), eslot=V((n_user, n_slot * chunk, cand), BF16),
        u2=V((2, rows, gw), BF16), q2=V((2, rows, gw), BF16),
        k2=V((2, n_key, gw), BF16), v2=V((2, n_key, gw), BF16),
        att=V((2, QB, gw), F32), catt=V((2, cand, gw), F32),
        pre_own=V((cand, 4 * d), F32), pre_slot=V((n_slot, cand, 2 * d), F32),
        uc=V((2, cand, gw), BF16), qc=V((2, cand, gw), BF16), gmix=V((cand, d), F32),
        gatt=V((2, cand, gw), BF16),
        wts=V((2, GROUP * cand, n_late), BF16), slope=V((2, GROUP * cand, n_key), F32),
        gq=V((2, cand, gw), F32), gkv=V((2, 2, n_late, gw), F32),
        dsend=V((n_user, n_slot * chunk, cand), BF16),
        drecv=V((n_user, n_slot * chunk, cand), BF16),
        share=V((n_item, piece, cand), BF16), share_in=V((n_item, piece, cand), BF16),
        csum=V((n_user, chunk, cand), BF16), fin=V((n_user, chunk, cand), BF16),
        tgv=V((piece, vb), F32),
        local_sem=dma((8,)),
        s_tab=dma((n_user,)), r_tab=dma((n_user,)),
        s_tag=dma((n_user,)), r_tag=dma((n_user,)),
        s_tagi=dma((n_item,)), r_tagi=dma((n_item,)),
        s_own=dma((n_item,)), r_own=dma((n_item,)),
        s_slot=dma((n_user,)), r_slot=dma((n_user,)),
        s_back=dma((n_user,)), r_back=dma((n_user,)),
        s_share=dma((n_item,)), r_share=dma((n_item,)),
        s_fin=dma((n_user,)), r_fin=dma((n_user,)),
    )
    names = list(scratch)

    def body(*refs):
        kernel(*refs[:11], **dict(zip(names, refs[11:])))

    hist_out, cand_out, tgrad = pl.pallas_call(
        body,
        out_shape=(
            V((rows, d), BF16), V((cand, d), BF16), V((piece, vb), F32),
        ),
        in_specs=[hbm] * 8,
        out_specs=(pl.BlockSpec(memory_space=pltpu.VMEM),) * 3,
        scratch_shapes=list(scratch.values()),
        compiler_params=pltpu.CompilerParams(
            collective_id=0, has_side_effects=True, vmem_limit_bytes=58 * 1024 * 1024),
    )(
        hist_len, cand_lists, cand_ids, item_table.T, history[0], w_in, w_out, grad_cand[0],
    )
    hist_out, cand_out, tgrad = hand_over(hist_out, cand_out, tgrad)
    return hist_out[None], cand_out[None], tgrad.T


def solution(mesh):
    in_specs = (
        P(("item", "user"), None, None),
        P(("item", "user")),
        P(("item", "user"), None),
        P(("item", "user"), None),
        P("user", "item"),
        P(),
        P(),
        P(("item", "user"), None, None),
    )
    out_specs = (
        P(("item", "user"), None, None),
        P(("item", "user"), None, None),
        P("user", "item"),
    )
    return jax.shard_map(local, mesh=mesh, in_specs=in_specs, out_specs=out_specs, check_vma=False)
```

```python
import functools

import jax
import jax.numpy as jnp
from jax import lax
from jax.experimental import pallas as pl
from jax.experimental.pallas import tpu as pltpu
from jax.sharding import PartitionSpec as P

H = 8
GROUP = 4
NORM_EPS = 1e-05
QB = 256
MESH = pl.DeviceIdType.MESH

F32 = jnp.float32
BF16 = jnp.bfloat16


def nn(a, b):
    return lax.dot_general(a, b, (((1,), (0,)), ((), ())), preferred_element_type=F32)


def nt(a, b):
    return lax.dot_general(a, b, (((1,), (1,)), ((), ())), preferred_element_type=F32)


def tn(a, b):
    return lax.dot_general(a, b, (((0,), (0,)), ((), ())), preferred_element_type=F32)


def silu(v):
    half = 0.5 * v
    return half + half * jnp.tanh(half)


def silu_slope(v):
    half = 0.5 * v
    sig = 0.5 + 0.5 * jnp.tanh(half)
    return sig + (v * sig) * (1.0 - sig)


def head_lane(shape, h):
    lane = lax.broadcasted_iota(jnp.int32, shape, len(shape) - 1)
    width = shape[-1] // GROUP
    return (lane >= h * width) & (lane < (h + 1) * width)


def only_head(x, h):
    return jnp.where(head_lane(x.shape, h), x, jnp.zeros_like(x))


def stacked_heads(x):
    return jnp.concatenate([only_head(x, h) for h in range(GROUP)], 0)


def unstacked_heads(x):
    rows = x.shape[0] // GROUP
    total = only_head(x[:rows], 0)
    for h in range(1, GROUP):
        total = total + only_head(x[h * rows : (h + 1) * rows], h)
    return total


def kernel(
    len_hbm, lists_hbm, ids_hbm, table_hbm, hist_hbm, win_hbm, wout_hbm, gcand_hbm,
    hist_out, cand_out, tgrad_out, *,
    len_ref, lists_ref, ids_ref, hist, win, wout, gcand, tabv, hold, tags, tags_i, pick, back, hotc, e_all, disp, eown, eslot,
    u2, q2, k2, v2, att, catt, pre_own, pre_slot, uc, qc, gmix, gatt, wts, slope, gq, gkv,
    dsend, drecv, share, share_in, csum, fin, tgv,
    local_sem, s_tab, r_tab, s_tag, r_tag, s_tagi, r_tagi, s_own, r_own, s_slot, r_slot,
    s_back, r_back, s_share, r_share, s_fin, r_fin,
):
    n_item = lax.axis_size("item")
    n_user = lax.axis_size("user")
    me_i = lax.axis_index("item")
    me_u = lax.axis_index("user")
    rows, d = hist.shape
    cand = gcand.shape[0]
    chunk = e_all.shape[1]
    piece, vb = tabv.shape
    per = piece // chunk
    gw = d // 2
    n_slot = eslot.shape[1] // chunk
    own_end = rows + cand
    scale = (d // H) ** (-0.5)
    barrier = pltpu.get_barrier_semaphore()
    def chunk_of(k):
        return lax.rem(k // per + n_item - me_i, n_item) * per + lax.rem(k, per)

    my_chunk = chunk_of(me_u)
    holder = my_chunk // per
    at_home = holder == me_i

    def peer_i(k):
        return {"item": lax.rem(me_i + k, n_item)}

    def peer_u(k):
        return {"user": lax.rem(me_u + k, n_user)}

    def worker(n):
        row = lax.rem(me_i + n // per, n_item)
        return (row, lax.rem(me_i + row, n_item) * per + lax.rem(n, per))

    def not_me(place):
        return jnp.logical_or(place[0] != me_i, place[1] != me_u)

    def signal(place):
        pl.semaphore_signal(barrier, inc=1, device_id=place, device_id_type=MESH)

    for k in range(1, n_item):
        signal(peer_i(k))
    for k in range(1, n_user):
        signal(peer_u(k))

    small = [
        pltpu.make_async_copy(len_hbm, len_ref, local_sem.at[0]),
        pltpu.make_async_copy(lists_hbm, lists_ref, local_sem.at[1]),
        pltpu.make_async_copy(ids_hbm, ids_ref, local_sem.at[2]),
        pltpu.make_async_copy(table_hbm, tabv, local_sem.at[3]),
    ]
    copies = [
        pltpu.make_async_copy(hist_hbm, hist, local_sem.at[4]),
        pltpu.make_async_copy(win_hbm, win, local_sem.at[5]),
        pltpu.make_async_copy(gcand_hbm, gcand, local_sem.at[6]),
        pltpu.make_async_copy(wout_hbm, wout, local_sem.at[7]),
    ]
    for c in small + copies:
        c.start()

    def build_tags():
        lane = lax.broadcasted_iota(jnp.int32, (1, cand), 1)
        key_row = jnp.zeros((1, cand), jnp.int32)
        for t in range(n_slot):
            key_row = jnp.where(lane // chunk == t, lists_ref[0, t] * chunk + lane - t * chunk, key_row)
        tag = jnp.concatenate([ids_ref[...], key_row, jnp.zeros((6, cand), jnp.int32)], 0)
        tags[me_u] = tag
        tags_i[me_i] = ids_ref[...]

    def remote(src, dst, send, recv, place):
        return pltpu.make_async_remote_copy(
            src_ref=src, dst_ref=dst, send_sem=send, recv_sem=recv, device_id=place,
            device_id_type=MESH)

    def tag_copy(k):
        return remote(tags.at[me_u], tags.at[me_u], s_tag.at[k], r_tag.at[k], peer_u(k))

    def tagi_copy(k):
        return remote(ids_hbm, tags_i.at[me_i], s_tagi.at[k], r_tagi.at[k], peer_i(k))

    def row_of(n):
        return lax.rem(me_i + n // per, n_item)

    def tab_copy(n):
        part = pl.ds((n % per) * chunk, chunk)
        return remote(hold.at[row_of(n), part], e_all.at[me_u], s_tab.at[n], r_tab.at[me_u],
                      worker(n))

    def tab_arrival(u):
        return remote(e_all.at[u], e_all.at[u], s_tab.at[u], r_tab.at[u], (holder, u))

    def own_copy(k):
        to = lax.rem(me_i + k, n_item)
        return remote(hold.at[to], eown.at[me_i], s_own.at[k], r_own.at[k], peer_i(k))

    def slot_copy(k):
        to = lax.rem(me_u + k, n_user)
        return remote(disp.at[to], eslot.at[my_chunk], s_slot.at[k], r_slot.at[k], peer_u(k))

    def back_copy(k):
        to = lax.rem(me_u + k, n_user)
        return remote(dsend.at[chunk_of(to)], drecv.at[me_u], s_back.at[k], r_back.at[k], peer_u(k))

    def share_copy(k):
        to = lax.rem(me_i + k, n_item)
        return remote(share.at[to], share_in.at[me_i], s_share.at[k], r_share.at[k], peer_i(k))

    def fin_copy(r):
        n = me_i * per + lax.rem(me_u, per)
        return remote(csum.at[r], fin.at[n], s_fin.at[r], r_fin.at[n], (holder, r))

    def fin_from(n):
        row = n // per
        return (row, lax.rem(me_i + row, n_item) * per + lax.rem(n, per))

    def fin_arrival(n):
        return remote(fin.at[n], fin.at[n], s_fin.at[n], r_fin.at[n], fin_from(n))

    pl.semaphore_wait(barrier, n_item + n_user - 2)

    @pl.loop(1, n_item)
    def _(k):
        tagi_copy(k).start()

    for c in small:
        c.wait()
    length = len_ref[0]
    build_tags()

    @pl.loop(1, n_user)
    def _(k):
        tag_copy(k).start()

    for c in copies:
        c.wait()

    def normalize(a0, a1):
        mean = (jnp.sum(a0, 1, keepdims=True) + jnp.sum(a1, 1, keepdims=True)) / d
        a0 = a0 - mean
        a1 = a1 - mean
        var = (jnp.sum(a0 * a0, 1, keepdims=True) + jnp.sum(a1 * a1, 1, keepdims=True)) / d
        inv = lax.rsqrt(var + NORM_EPS)
        return a0 * inv, a1 * inv, inv

    def history_block(b):
        lo = b * QB
        n = lo + QB

        @pl.loop(0, 2)
        def _(g):
            q = q2[g, lo:n]
            key = k2[g, :n]
            val = v2[g, :n]
            total = jnp.zeros((QB, gw), F32)
            for h in range(GROUP):
                y = nt(only_head(q, h), key)
                w = y + y * jnp.tanh(y)
                last = w[:, lo:]
                r = lax.broadcasted_iota(jnp.int32, (QB, QB), 0)
                c = lax.broadcasted_iota(jnp.int32, (QB, QB), 1)
                last = jnp.where(c <= r, last, 0.0).astype(BF16)
                if b:
                    w = jnp.concatenate([w[:, :lo].astype(BF16), last], 1)
                else:
                    w = last
                total = total + only_head(nn(w, val), h)
            att[g] = total

        n0, n1, _ = normalize(att[0], att[1])
        m0 = (n0 * u2[0, lo:n].astype(F32)).astype(BF16)
        m1 = (n1 * u2[1, lo:n].astype(F32)).astype(BF16)
        out = nn(m0, wout[:gw]) + nn(m1, wout[gw:]) + hist[lo:n].astype(F32)
        keep = (lo + lax.broadcasted_iota(jnp.int32, (QB, 1), 0)) < length
        hist_out[lo:n] = jnp.where(keep, out, 0.0).astype(BF16)

    def project(b):
        at = pl.ds(pl.multiple_of(b * QB, QB), QB)
        x = hist[at]
        keep = (b * QB + lax.broadcasted_iota(jnp.int32, (QB, 1), 0)) < length
        for g in range(2):
            c = g * gw
            u2[g, at] = silu(nn(x, win[:, c : c + gw])).astype(BF16)
            val = silu(nn(x, win[:, d + c : d + c + gw]))
            v2[g, at] = jnp.where(keep, val, 0.0).astype(BF16)
            q2[g, at] = silu(nn(x, win[:, 2 * d + c : 2 * d + c + gw])).astype(BF16) * (scale / 2)
            k2[g, at] = silu(nn(x, win[:, 3 * d + c : 3 * d + c + gw])).astype(BF16)

    half = rows // QB // 2
    pl.loop(0, half)(project)

    at = lax.broadcasted_iota(jnp.int32, (vb, cand), 0)
    for j in range(n_item):
        i = lax.rem(me_i + j, n_item)
        if j:
            tagi_copy(n_item - j).wait_recv()
        hot = jnp.where(at == tags_i[i], 1.0, 0.0).astype(BF16)
        hold[i] = nn(tabv[...], hot).astype(BF16)
        for n in range(j * per, (j + 1) * per):
            @pl.when(not_me(worker(n)))
            def _():
                tab_copy(n).start()
        if j:
            own_copy(j).start()

    @pl.when(at_home)
    def _():
        part = pl.ds(pl.multiple_of(lax.rem(me_u, per) * chunk, chunk), chunk)
        e_all[me_u] = hold[me_i, part]

    eown[me_i] = hold[me_i]
    pl.loop(half, rows // QB)(project)

    @pl.loop(1, n_user)
    def _(k):
        tag_copy(k).wait_recv()

    keys = jnp.concatenate([tags[u, 1:2] for u in range(n_user)], 0)
    keys_t = jnp.transpose(keys.astype(F32)).astype(jnp.int32)
    line = n_slot * chunk
    col = lax.broadcasted_iota(jnp.int32, (line, n_user * chunk), 1)
    for u in range(n_user):
        pick[u * line : (u + 1) * line] = jnp.where(
            col == keys_t[:, u : u + 1], 1.0, 0.0).astype(BF16)

    history_block(0)

    @pl.loop(0, n_user)
    def _(u):
        @pl.when(not_me((holder, u)))
        def _():
            tab_arrival(u).wait_recv()

    picked = nn(pick[...], e_all[...].reshape(n_user * chunk, cand)).astype(BF16)
    disp[...] = picked.reshape(disp.shape)
    eslot[my_chunk] = disp[me_u]

    @pl.loop(1, n_user)
    def _(k):
        slot_copy(k).start()

    row = lax.broadcasted_iota(jnp.int32, (n_user * chunk, line), 0)
    for u in range(n_user):
        back[:, u * line : (u + 1) * line] = jnp.where(
            row == tags[u, 1:2], 1.0, 0.0).astype(BF16)

    @pl.loop(1, n_item)
    def _(k):
        own_copy(k).wait_recv()

    own = jnp.transpose(eown[...].reshape(d, cand).astype(F32)).astype(BF16)
    pre_own[...] = nn(own, win[...])
    for g in range(2):
        c = g * gw
        uc[g] = silu(pre_own[:, c : c + gw]).astype(BF16)
        v2[g, rows:own_end] = silu(pre_own[:, d + c : d + c + gw]).astype(BF16)
        qc[g] = silu(pre_own[:, 2 * d + c : 2 * d + c + gw]).astype(BF16) * (scale / 2)
        k2[g, rows:own_end] = silu(pre_own[:, 3 * d + c : 3 * d + c + gw]).astype(BF16)

    def scores(g, lo, hi):
        y = nt(stacked_heads(qc[g]), k2[g, lo:hi])
        t = jnp.tanh(y)
        w = y + y * t
        p = 0.5 + 0.5 * t
        slope[g, :, lo:hi] = p + w * (1.0 - p)
        wb = w.astype(BF16)
        late = max(lo, rows)
        wts[g, :, late - rows : hi - rows] = wb[:, late - lo :]
        return unstacked_heads(nn(wb, v2[g, lo:hi]))

    @pl.loop(0, 2)
    def _(g):
        catt[g] = scores(g, 0, own_end)

    history_block(2)
    gmix[...] = nt(gcand[...], wout[...])

    @pl.loop(1, n_user)
    def _(k):
        slot_copy(k).wait_recv()

    for t in range(n_slot):
        e = eslot[:, t * chunk : (t + 1) * chunk].reshape(d, cand)
        e = jnp.transpose(e.astype(F32)).astype(BF16)
        at = pl.ds(own_end + t * cand, cand)
        for g in range(2):
            c = g * gw
            pv = nn(e, win[:, d + c : d + c + gw])
            pk = nn(e, win[:, 3 * d + c : 3 * d + c + gw])
            pre_slot[t, :, c : c + gw] = pv
            pre_slot[t, :, d + c : d + c + gw] = pk
            v2[g, at] = silu(pv).astype(BF16)
            k2[g, at] = silu(pk).astype(BF16)

    n_key = k2.shape[1]

    @pl.loop(0, 2)
    def _(g):
        catt[g] += scores(g, own_end, n_key)

    n0, n1, inv = normalize(catt[0], catt[1])
    uc0 = uc[0].astype(F32)
    uc1 = uc[1].astype(F32)
    gm0 = gmix[:, :gw]
    gm1 = gmix[:, gw:]
    gn0 = gm0 * uc0
    gn1 = gm1 * uc1
    mean_g = (jnp.sum(gn0, 1, keepdims=True) + jnp.sum(gn1, 1, keepdims=True)) / d
    mean_gn = (jnp.sum(gn0 * n0, 1, keepdims=True) + jnp.sum(gn1 * n1, 1, keepdims=True)) / d
    gatt[0] = (inv * (gn0 - mean_g - n0 * mean_gn)).astype(BF16)
    gatt[1] = (inv * (gn1 - mean_g - n1 * mean_gn)).astype(BF16)
    gmix[:, :gw] = gm0 * n0
    gmix[:, gw:] = gm1 * n1
    m0 = (n0 * uc0).astype(BF16)
    m1 = (n1 * uc1).astype(BF16)

    def score_grads(g, lo, hi):
        ga = stacked_heads(gatt[g])
        gs = (nt(ga, v2[g, lo:hi]) * slope[g, :, lo:hi] * scale).astype(BF16)
        late = max(lo, rows)
        gkv[0, g, late - rows : hi - rows] = tn(
            gs[:, late - lo :], stacked_heads(qc[g])) * (2.0 / scale)
        gkv[1, g, late - rows : hi - rows] = tn(wts[g, :, late - rows : hi - rows], ga)
        return unstacked_heads(nn(gs, k2[g, lo:hi]))

    @pl.loop(0, 2)
    def _(g):
        gq[g] = score_grads(g, own_end, n_key)

    for t in range(n_slot):
        at = pl.ds(cand + t * cand, cand)
        total = jnp.zeros((d, cand), F32)
        for g in range(2):
            c = g * gw
            dk = (gkv[0, g, at] * silu_slope(pre_slot[t, :, d + c : d + c + gw])).astype(BF16)
            dv = (gkv[1, g, at] * silu_slope(pre_slot[t, :, c : c + gw])).astype(BF16)
            total = total + nt(win[:, d + c : d + c + gw], dv)
            total = total + nt(win[:, 3 * d + c : 3 * d + c + gw], dk)
        dsend[:, t * chunk : (t + 1) * chunk] = total.astype(BF16).reshape(n_user, chunk, cand)

    drecv[me_u] = dsend[my_chunk]

    @pl.loop(1, n_user)
    def _(k):
        back_copy(k).start()

    cand_out[...] = (nn(m0, wout[:gw]) + nn(m1, wout[gw:]) + own.astype(F32)).astype(BF16)

    @pl.loop(0, 2)
    def _(g):
        gq[g] += score_grads(g, 0, own_end)

    total = jnp.transpose(gcand[...].astype(F32))
    for g in range(2):
        c = g * gw
        for part, grad in (
            (0, gmix[:, c : c + gw]),
            (1, gkv[1, g, :cand]),
            (2, gq[g]),
            (3, gkv[0, g, :cand]),
        ):
            cl = part * d + c
            dp = (grad * silu_slope(pre_own[:, cl : cl + gw])).astype(BF16)
            total = total + nt(win[:, cl : cl + gw], dp)
    share[...] = total.astype(BF16).reshape(share.shape)
    share_in[me_i] = share[me_i]

    @pl.loop(1, n_item)
    def _(k):
        share_copy(k).start()

    history_block(3)

    @pl.loop(1, n_user)
    def _(k):
        back_copy(k).wait_recv()

    summed = nn(back[...], drecv[...].reshape(n_user * line, cand)).astype(BF16)
    csum[...] = summed.reshape(csum.shape)

    @pl.loop(0, n_user)
    def _(r):
        @pl.when(not_me((holder, r)))
        def _():
            fin_copy(r).start()

    @pl.when(at_home)
    def _():
        fin[me_i * per + lax.rem(me_u, per)] = csum[me_u]

    history_block(1)

    @pl.loop(1, n_item)
    def _(k):
        share_copy(k).wait_recv()

    ids_t = jnp.concatenate([tags_i[i] for i in range(n_item)], 0)
    ids_t = jnp.transpose(ids_t.astype(F32)).astype(jnp.int32)
    col = lax.broadcasted_iota(jnp.int32, (cand, vb), 1)
    for i in range(n_item):
        hotc[i] = jnp.where(col == ids_t[:, i : i + 1], 1.0, 0.0).astype(BF16)
    hot_all = hotc[...].reshape(n_item * cand, vb)
    tgv[...] = nn(jnp.concatenate([share_in[i] for i in range(n_item)], 1), hot_all)

    @pl.loop(0, n_user)
    def _(n):
        @pl.when(not_me(fin_from(n)))
        def _():
            fin_arrival(n).wait_recv()

    terms = [fin[i * per : (i + 1) * per].reshape(piece, cand) for i in range(n_item)]
    tgrad_out[...] = tgv[...] + nn(jnp.concatenate(terms, 1), hot_all)

    @pl.loop(1, n_item)
    def _(k):
        tagi_copy(k).wait_send()
        own_copy(k).wait_send()
        share_copy(k).wait_send()

    @pl.loop(1, n_user)
    def _(k):
        tag_copy(k).wait_send()
        slot_copy(k).wait_send()
        back_copy(k).wait_send()

    @pl.loop(0, n_user)
    def _(n):
        @pl.when(not_me(worker(n)))
        def _():
            tab_copy(n).wait_send()

        @pl.when(not_me((holder, n)))
        def _():
            fin_copy(n).wait_send()


def hand_over_kernel(a, b, c, a_out, b_out, c_out, sem):
    moves = [
        pltpu.make_async_copy(x, y, sem.at[j])
        for j, (x, y) in enumerate(((a, a_out), (b, b_out), (c, c_out)))
    ]
    for m in moves:
        m.start()
    for m in moves:
        m.wait()


def hand_over(*arrays):
    hbm = pl.BlockSpec(memory_space=pl.ANY)
    return pl.pallas_call(
        hand_over_kernel,
        out_shape=tuple(jax.ShapeDtypeStruct(x.shape, x.dtype) for x in arrays),
        in_specs=[hbm] * 3,
        out_specs=(hbm,) * 3,
        scratch_shapes=[pltpu.SemaphoreType.DMA((3,))],
        compiler_params=pltpu.CompilerParams(vmem_limit_bytes=1024 * 1024),
    )(*arrays)


def local(history, hist_len, cand_ids, cand_lists, item_table, w_in, w_out, grad_cand):
    rows, d = history.shape[1:]
    cand = cand_ids.shape[1]
    n_slot = cand_lists.shape[1]
    vb, piece = item_table.shape
    n_item = lax.axis_size("item")
    n_user = lax.axis_size("user")
    gw = d // 2
    chunk = d // n_user
    n_late = (1 + n_slot) * cand
    n_key = rows + n_late
    hbm = pl.BlockSpec(memory_space=pl.ANY)
    V = pltpu.VMEM
    dma = pltpu.SemaphoreType.DMA
    scratch = dict(
        len_ref=pltpu.SMEM((1,), jnp.int32), lists_ref=pltpu.SMEM((1, n_slot), jnp.int32),
        ids_ref=V((1, cand), jnp.int32),
        hist=V((rows, d), BF16), win=V((d, 4 * d), BF16), wout=V((d, d), BF16),
        gcand=V((cand, d), BF16),
        tabv=V((piece, vb), BF16), hold=V((n_item, piece, cand), BF16),
        tags=V((n_user, 8, cand), jnp.int32), tags_i=V((n_item, 1, cand), jnp.int32),
        pick=V((n_user * n_slot * chunk, n_user * chunk), BF16),
        back=V((n_user * chunk, n_user * n_slot * chunk), BF16),
        hotc=V((n_item, cand, vb), BF16),
        e_all=V((n_user, chunk, cand), BF16), disp=V((n_user, n_slot * chunk, cand), BF16),
        eown=V((n_item, piece, cand), BF16), eslot=V((n_user, n_slot * chunk, cand), BF16),
        u2=V((2, rows, gw), BF16), q2=V((2, rows, gw), BF16),
        k2=V((2, n_key, gw), BF16), v2=V((2, n_key, gw), BF16),
        att=V((2, QB, gw), F32), catt=V((2, cand, gw), F32),
        pre_own=V((cand, 4 * d), F32), pre_slot=V((n_slot, cand, 2 * d), F32),
        uc=V((2, cand, gw), BF16), qc=V((2, cand, gw), BF16), gmix=V((cand, d), F32),
        gatt=V((2, cand, gw), BF16),
        wts=V((2, GROUP * cand, n_late), BF16), slope=V((2, GROUP * cand, n_key), F32),
        gq=V((2, cand, gw), F32), gkv=V((2, 2, n_late, gw), F32),
        dsend=V((n_user, n_slot * chunk, cand), BF16),
        drecv=V((n_user, n_slot * chunk, cand), BF16),
        share=V((n_item, piece, cand), BF16), share_in=V((n_item, piece, cand), BF16),
        csum=V((n_user, chunk, cand), BF16), fin=V((n_user, chunk, cand), BF16),
        tgv=V((piece, vb), F32),
        local_sem=dma((8,)),
        s_tab=dma((n_user,)), r_tab=dma((n_user,)),
        s_tag=dma((n_user,)), r_tag=dma((n_user,)),
        s_tagi=dma((n_item,)), r_tagi=dma((n_item,)),
        s_own=dma((n_item,)), r_own=dma((n_item,)),
        s_slot=dma((n_user,)), r_slot=dma((n_user,)),
        s_back=dma((n_user,)), r_back=dma((n_user,)),
        s_share=dma((n_item,)), r_share=dma((n_item,)),
        s_fin=dma((n_user,)), r_fin=dma((n_user,)),
    )
    names = list(scratch)

    def body(*refs):
        kernel(*refs[:11], **dict(zip(names, refs[11:])))

    hist_out, cand_out, tgrad = pl.pallas_call(
        body,
        out_shape=(
            V((rows, d), BF16), V((cand, d), BF16), V((piece, vb), F32),
        ),
        in_specs=[hbm] * 8,
        out_specs=(pl.BlockSpec(memory_space=pltpu.VMEM),) * 3,
        scratch_shapes=list(scratch.values()),
        compiler_params=pltpu.CompilerParams(
            collective_id=0, has_side_effects=True, vmem_limit_bytes=58 * 1024 * 1024),
    )(
        hist_len, cand_lists, cand_ids, item_table.T, history[0], w_in, w_out, grad_cand[0],
    )
    hist_out, cand_out, tgrad = hand_over(hist_out, cand_out, tgrad)
    return hist_out[None], cand_out[None], tgrad.T


def solution(mesh):
    in_specs = (
        P(("item", "user"), None, None),
        P(("item", "user")),
        P(("item", "user"), None),
        P(("item", "user"), None),
        P("user", "item"),
        P(),
        P(),
        P(("item", "user"), None, None),
    )
    out_specs = (
        P(("item", "user"), None, None),
        P(("item", "user"), None, None),
        P("user", "item"),
    )
    return jax.shard_map(local, mesh=mesh, in_specs=in_specs, out_specs=out_specs, check_vma=False)
```
